32 devices in a mesh: parts: 2 (over y), view: 4 (over x, core), tile: 4 (over z).
Axes of the slice: x: 2, y: 2, z: 4, core: 2. Of those that a mesh axis runs over, the one named last changes fastest.
Arguments:
- data: float32 [8, 32, 48, 32], P(('parts', 'view'), 'tile'), parts along dimension 0, may hold values from 0.25 to 4
- labels: int32 [8, 32, 48, 32], P(('parts', 'view'), 'tile'), parts along dimension 0, may hold values from 0 to 3
- kernel: float32 [4, 32, 9], P('view'), may hold values from 0.1 to 1
- offsets: int32 [4, 32], P('view'), may hold values from -2 to 2
Outputs:
- estimate: float32 [8, 32, 48, 32], P(('parts', 'view'), 'tile'), parts along dimension 0
The draws below stay inside these ranges and needn't reach their ends.
There are 2 independent parts, one for each index of `parts`. The reference program is written for one: setup_inputs(seed, part) draws one part's arguments, and reference() takes and returns one part's arrays. A program takes and returns all parts, laid end to end along the dimension named above; an argument that names none is the same for every part. Nothing has to cross between parts.
All inputs are finite; a program needn't handle non-finite values.
Results may differ from the reference program's by a relative error of at most 0.000088.
Values sent between devices are 32-bit elements; how exact they have to be, the bound alone decides.
No kernel may reach another device: no remote copies, remote signals or barrier semaphores. Data moves between devices by JAX's collectives and lax.ppermute only.
A program may use at most 64 MiB of HBM per device.

```python
import math
import jax
import jax.numpy as jnp
from jax import lax

Y = 48
ITERS = 2
SWEEPS = 4
TAPS = 9
VIEWS = 4
X = 32
Z = 32


def plant(array, rng, smallest, top_value):
    shape = array.shape
    index_at = [jax.random.randint(jax.random.fold_in(rng, axis), (), 0, shape[axis]) for axis in range(len(shape))]
    array = array.at[tuple(index_at)].set(smallest)
    longest = shape.index(max(shape))
    index_at[longest] = (index_at[longest] + 1) % shape[longest]
    return array.at[tuple(index_at)].set(top_value)


def block_scale(own_key, extent, cuts, smallest, top_value):
    def one(dim, blocks):
        draws = jax.random.uniform(jax.random.fold_in(jax.random.fold_in(own_key, 6), dim), (blocks,), jnp.float32, smallest / len(cuts), top_value / len(cuts))
        return jnp.repeat(jnp.exp(draws), extent[dim] // blocks).reshape((-1,) + (1,) * (len(extent) - dim - 1))

    level = one(*cuts[0])
    for cut in cuts[1:]:
        level = level * one(*cut)
    return level


def setup_inputs(seed: int = 0, part: int = 0) -> dict:
    key_list = jax.random.split(jax.random.key(seed), 5)
    part_splits = jax.random.split(jax.random.fold_in(key_list[4], part), 5)
    return {
        "data": jnp.clip(jnp.exp(math.log(4.0) - 2.7725887 * jax.random.uniform(part_splits[0], (VIEWS, X, Y, Z), jnp.float32) ** block_scale(part_splits[0], (VIEWS, X, Y, Z), ((0, 4), (1, 4)), -0.2, 0.2)), 0.25, 4.0),
        "labels": plant(jax.random.randint(part_splits[1], (VIEWS, X, Y, Z), 0, 4), jax.random.fold_in(part_splits[1], 1), 0, 3).astype(jnp.int32),
        "kernel": jnp.clip(jnp.exp(math.log(1.0) - 2.3025851 * jax.random.uniform(key_list[2], (VIEWS, Z, TAPS), jnp.float32) ** block_scale(key_list[2], (VIEWS, Z, TAPS), ((0, 4),), -0.2, 0.2)), 0.1, 1.0),
        "offsets": plant(jax.random.randint(key_list[3], (VIEWS, Z), -2, 3), jax.random.fold_in(key_list[3], 1), -2, 2).astype(jnp.int32),
    }


WEAK = 0.2
TAU = 0.15

def band(kernel, offsets):
    depth_cells = kernel.shape[0]
    taps = jnp.arange(kernel.shape[1], dtype=jnp.int32) - 4
    depth = jnp.arange(depth_cells, dtype=jnp.int32)
    index = jnp.clip(depth[:, None] + taps[None, :] + offsets[:, None], 0, depth_cells - 1).astype(jnp.int32)
    weight = kernel / lax.optimization_barrier(jnp.sum(kernel, axis=1, keepdims=True))
    return (index, weight)

def blur_taps(field, index, weight):
    total = jnp.zeros_like(field)
    for k in range(index.shape[1]):
        total = total + jnp.take(field, index[:, k], axis=2) * weight[:, k]
    return total

def adjoint_taps(ratio, index, weight):
    total = jnp.zeros_like(ratio)
    for k in range(index.shape[1]):
        total = total.at[:, :, index[:, k]].add(ratio * weight[:, k])
    return total

def axis_term(field, region, axis):
    count = field.shape[axis]
    upper = lax.slice_in_dim(field, 1, count, axis=axis)
    lower = lax.slice_in_dim(field, 0, count - 1, axis=axis)
    same = jnp.where(lax.slice_in_dim(region, 1, count, axis=axis) == lax.slice_in_dim(region, 0, count - 1, axis=axis), 1.0, WEAK)
    flux = same * (upper - lower)
    after = [(0, 0)] * 3
    before = [(0, 0)] * 3
    after[axis] = (0, 1)
    before[axis] = (1, 0)
    return jnp.pad(flux, after) - jnp.pad(flux, before)

def sweep_whole(field, region):
    total = axis_term(field, region, 0) + axis_term(field, region, 1) + axis_term(field, region, 2)
    return field + TAU * total

def reference(data, labels, kernel, offsets):
    bands = [band(kernel[v], offsets[v]) for v in range(VIEWS)]
    current = [data[v] for v in range(VIEWS)]
    for step in range(ITERS):
        correction = [adjoint_taps(data[v] / blur_taps(current[v], *bands[v]), *bands[v]) for v in range(VIEWS)]
        paired = [jnp.sqrt(correction[v] * jnp.rot90(correction[(v + 2) % 4], 2, axes=(0, 2))) for v in range(VIEWS)]
        joined = [jnp.sqrt(paired[v] * jnp.rot90(paired[v ^ 1], 3 if v % 2 == 0 else 1, axes=(0, 2))) for v in range(VIEWS)]
        current = [current[v] * joined[v] for v in range(VIEWS)]
        for sweep in range(SWEEPS):
            current = [sweep_whole(current[v], labels[v]) for v in range(VIEWS)]
    return jnp.stack(current)
```

```python
import functools

import jax
import jax.experimental.pallas as pl
import jax.experimental.pallas.tpu as pltpu
import jax.numpy as jnp
from jax import lax
from jax.sharding import PartitionSpec as P

ITERS = 2
SWEEPS = 4

WEAK = 0.2
TAU = 0.15

LANES = 128
ROWS = 8
VIEWS = 4


def extended(cells, sides, width):
    for axis, dim in sides:
        count = lax.axis_size(axis)
        ends = count - 1
        head = lax.slice_in_dim(cells, 0, width, axis=dim)
        tail = lax.slice_in_dim(cells, cells.shape[dim] - width, cells.shape[dim], axis=dim)
        cells = jnp.concatenate(
            [
                lax.ppermute(tail, axis, [(i, (i + 1) % count) for i in range(ends)]),
                cells,
                lax.ppermute(head, axis, [((i + 1) % count, i) for i in range(ends)]),
            ],
            axis=dim,
        )
    return cells


def swapped(block, axis, stride):
    count = lax.axis_size(axis)
    route = []
    for low in range(count):
        high = low | 1 << stride
        if high != low and high < count:
            route += [(low, high), (high, low)]
    return lax.ppermute(block, axis, route)


def band(kernel, offsets):
    depth_cells = kernel.shape[0]
    taps = jnp.arange(kernel.shape[1], dtype=jnp.int32) - 4
    depth = jnp.arange(depth_cells, dtype=jnp.int32)
    index = jnp.clip(depth[:, None] + taps[None, :] + offsets[:, None], 0, depth_cells - 1)
    weight = kernel / jnp.sum(kernel, axis=1, keepdims=True)
    return (index, weight)


def axis_term(field, region, axis):
    count = field.shape[axis]
    upper = lax.slice_in_dim(field, 1, count, axis=axis)
    lower = lax.slice_in_dim(field, 0, count - 1, axis=axis)
    same = jnp.where(
        lax.slice_in_dim(region, 1, count, axis=axis)
        == lax.slice_in_dim(region, 0, count - 1, axis=axis),
        1.0,
        WEAK,
    )
    flux = same * (upper - lower)
    after = [(0, 0)] * 3
    before = [(0, 0)] * 3
    after[axis] = (0, 1)
    before[axis] = (1, 0)
    return jnp.pad(flux, after) - jnp.pad(flux, before)


def sweep_rows(field, region, first_row, total_rows):
    extent = field.shape[0]
    global_rows = first_row + jnp.arange(extent, dtype=jnp.int32)
    inside = ((global_rows >= 0) & (global_rows < total_rows)).astype(field.dtype)[:, None, None]
    same = jnp.where(region[1:] == region[:-1], 1.0, WEAK) * inside[1:] * inside[:-1]
    flux = same * (field[1:] - field[:-1])
    inner = field[1:-1]
    inner_labels = region[1:-1]
    total = (
        flux[1:] - flux[:-1] + axis_term(inner, inner_labels, 1) + axis_term(inner, inner_labels, 2)
    )
    return inner + TAU * total


def regroup(received, tiles):
    slab, rows, depth_cells = received.shape
    blocks = received.reshape(slab, rows, tiles, depth_cells // tiles)
    return blocks.transpose(3, 1, 2, 0).reshape(depth_cells // tiles, rows, depth_cells)


def by_slabs(data, labels, kernel, offsets):
    recorded = data[0]
    region = labels[0]
    index, weight = band(kernel[0], offsets[0])
    tiles = lax.axis_size("tile")
    slab, rows, depth_cells = recorded.shape
    total_rows = slab * tiles
    start = lax.axis_index("tile") * slab
    parity = lax.axis_index("view") % 2
    columns = jnp.arange(depth_cells, dtype=jnp.int32)
    matrix = jnp.sum(weight[:, :, None] * (index[:, :, None] == columns[None, None, :]), axis=1)
    label_ext = extended(region, (("tile", 0),), SWEEPS)
    views = lax.axis_size("view")
    half_turn = [
        (v * tiles + t, (v + 2) % views * tiles + tiles - 1 - t)
        for v in range(views)
        for t in range(tiles)
    ]
    current = recorded
    for step in range(ITERS):
        forward_flat = jnp.dot(
            current.reshape(-1, depth_cells), matrix.T, precision=lax.Precision.HIGHEST
        )
        field = recorded / forward_flat.reshape(current.shape)
        flat = jnp.dot(field.reshape(-1, depth_cells), matrix, precision=lax.Precision.HIGHEST)
        correction = flat.reshape(field.shape)
        turned = jnp.flip(lax.ppermute(correction, ("view", "tile"), half_turn), (0, 2))
        paired = jnp.sqrt(correction * turned)
        outgoing = jnp.where(parity == 0, jnp.flip(paired, 2), paired)
        rotated = regroup(
            lax.all_to_all(outgoing, "tile", split_axis=2, concat_axis=2, tiled=True), tiles
        )
        rotated = jnp.where(parity == 1, jnp.flip(rotated, 2), rotated)
        partner = swapped(rotated, "view", 0)
        current = current * jnp.sqrt(paired * partner)
        widened = extended(current, (("tile", 0),), SWEEPS)
        for sweep in range(SWEEPS):
            extent = widened.shape[0]
            widened = sweep_rows(
                widened,
                label_ext[sweep : sweep + extent],
                start - SWEEPS + sweep,
                total_rows,
            )
        current = widened
    return current[None]


def rows_reversed():
    v = lax.axis_index("view")
    return lax.rem(v + 1, VIEWS) >= 2


def depth_reversed():
    return lax.axis_index("view") >= 2


def own_slot(tiles):
    t = lax.axis_index("tile")
    return jnp.where(rows_reversed(), tiles - 1 - t, t)


def lane_order(shape, depth_cells):
    lane = lax.broadcasted_iota(jnp.int32, shape, 1)
    base = lane // depth_cells * depth_cells
    return jnp.where(depth_reversed(), base + (base + depth_cells - 1 - lane), lane)


def pack_one(source, held, target, groups):
    slab, rows, depth_cells = held.shape
    turn = rows_reversed()
    for i in range(slab):
        held[i] = source[0, jnp.where(turn, slab - 1 - i, i)]
    part = rows // groups
    cells = jnp.swapaxes(held[...], 0, 1)
    cells = jnp.concatenate([cells[g * part : (g + 1) * part] for g in range(groups)], axis=2)
    flat = cells.reshape(part * slab, groups * depth_cells)
    order = lane_order(flat.shape, depth_cells)
    flat = jnp.take_along_axis(flat, order, axis=1)
    target[...] = flat.reshape(target.shape)


def pack_kernel(groups, data, labels, data_out, labels_out, held, held_labels):
    pack_one(data, held, data_out, groups)
    pack_one(labels, held_labels, labels_out, groups)


def band_kernel(kernel, offsets, band_out):
    depth_cells, taps = kernel.shape[1:]
    span = band_out.shape[0]
    turn = depth_reversed()
    row = lax.broadcasted_iota(jnp.int32, (depth_cells, depth_cells), 0)
    col = lax.broadcasted_iota(jnp.int32, (depth_cells, depth_cells), 1)
    pick = col == jnp.where(turn, depth_cells - 1 - row, row)
    shift = jnp.sum(
        jnp.where(pick, jnp.broadcast_to(offsets[...], pick.shape), 0), axis=1, keepdims=True
    )
    depth = row[:, :1]
    depth = jnp.where(turn, depth_cells - 1 - depth, depth)
    taps_by_row = jnp.dot(
        pick.astype(jnp.float32),
        kernel[0],
        precision=lax.Precision.HIGHEST,
        preferred_element_type=jnp.float32,
    )
    weight = taps_by_row / jnp.sum(taps_by_row, axis=1, keepdims=True)
    lane = lax.broadcasted_iota(jnp.int32, (depth_cells, span), 1)
    within = lax.rem(lane, depth_cells)
    within = jnp.where(turn, depth_cells - 1 - within, within)
    total = jnp.zeros((depth_cells, span), jnp.float32)
    for k in range(taps):
        index = jnp.clip(depth + (k - 4) + shift, 0, depth_cells - 1)
        total = total + jnp.where(index == within, weight[:, k : k + 1], 0.0)
    for g in range(span // depth_cells):
        mine = lane // depth_cells == g
        band_out[g * depth_cells : (g + 1) * depth_cells, :] = jnp.where(mine, total, 0.0)


def corrected(recorded, estimate, matrix):
    blurred = lax.dot_general(
        estimate,
        matrix,
        (((1,), (1,)), ((), ())),
        precision=lax.Precision.HIGHEST,
        preferred_element_type=jnp.float32,
    )
    return jnp.dot(
        recorded / blurred,
        matrix,
        precision=lax.Precision.HIGHEST,
        preferred_element_type=jnp.float32,
    )


def first_kernel(tiles, band_in, *refs):
    blocks, (whole, correction) = refs[:tiles], refs[tiles:]
    slot = own_slot(tiles)
    matrix = band_in[...]
    part, slab, lanes = blocks[0].shape
    for k in range(tiles):
        block = blocks[k][...]
        at = pl.ds(pl.multiple_of((slot ^ k) * slab, slab), slab)
        whole[:, at, :] = block
        flat = block.reshape(part * slab, lanes)
        correction[:, at, :] = corrected(flat, flat, matrix).reshape(block.shape)


def edges_kernel(tiles, depth_cells, *refs):
    blocks, (along_x, along_y, along_z, whole) = refs[:tiles], refs[tiles:]
    slot = own_slot(tiles)
    part, slab, lanes = blocks[0].shape
    for k in range(tiles):
        at = pl.ds(pl.multiple_of((slot ^ k) * slab, slab), slab)
        whole[:, at, :] = blocks[k][...]
    total_rows = tiles * slab
    region = whole[...].reshape(part * total_rows, lanes)
    row = lax.broadcasted_iota(jnp.int32, region.shape, 0)
    lane = lax.broadcasted_iota(jnp.int32, region.shape, 1)

    def weighted(upper, inside, target):
        same = jnp.where(upper == region, TAU, TAU * WEAK)
        target[...] = jnp.where(inside, same, 0.0).reshape(target.shape)

    weighted(up_rows(region), lax.rem(row, total_rows) != total_rows - 1, along_x)
    weighted(
        up_second(region, total_rows, depth_cells),
        (row < (part - 1) * total_rows) | (lane < lanes - depth_cells),
        along_y,
    )
    weighted(up_depth(region), lax.rem(lane, depth_cells) != depth_cells - 1, along_z)


def up_rows(cells):
    return pltpu.roll(cells, cells.shape[0] - 1, 0)


def up_depth(cells):
    return pltpu.roll(cells, cells.shape[1] - 1, 1)


def up_second(cells, total_rows, depth_cells):
    first = pltpu.roll(cells[:total_rows], cells.shape[1] - depth_cells, 1)
    return jnp.concatenate([cells[total_rows:], first], axis=0)


def down_second(cells, total_rows, depth_cells):
    last = pltpu.roll(cells[-total_rows:], depth_cells, 1)
    return jnp.concatenate([last, cells[:-total_rows]], axis=0)


def swept(cells, along_x, along_y, along_z, total_rows, depth_cells):
    flux_x = along_x * (up_rows(cells) - cells)
    flux_y = along_y * (up_second(cells, total_rows, depth_cells) - cells)
    flux_z = along_z * (up_depth(cells) - cells)
    return (
        cells
        + (flux_x - pltpu.roll(flux_x, 1, 0))
        + (flux_y - down_second(flux_y, total_rows, depth_cells))
        + (flux_z - pltpu.roll(flux_z, 1, 1))
    )


def exchanged(cells, depth_cells):
    part, rows, lanes = cells.shape
    groups = lanes // depth_cells
    lane_group = lax.broadcasted_iota(jnp.int32, (rows, lanes), 1) // depth_cells
    out = []
    for first in range(0, part, groups):
        turned = cells[first : first + groups].reshape(groups * rows, lanes).T
        for a in range(groups):
            plane = None
            for b in range(groups):
                piece = turned[b * rows : (b + 1) * rows]
                moved = (b - a) % groups * depth_cells
                if moved:
                    piece = pltpu.roll(piece, moved, 1)
                plane = piece if plane is None else jnp.where(lane_group == b, piece, plane)
            out.append(plane)
    return jnp.stack(out)


def product_kernel(depth_cells, own, other, product):
    product[...] = own[...] * exchanged(other[...], depth_cells)


def window(ref, slot, tiles, slab, margin):
    parts = []
    for step in (-1, 0, 1):
        at = lax.rem(slot + step + tiles, tiles) * slab
        parts.append(ref[:, pl.ds(pl.multiple_of(at, slab), slab), :])
    return jnp.concatenate(parts, axis=1)[:, slab - margin : 2 * slab + margin, :]


def second_kernel(
    depth_cells, band_in, recorded, product, received, along_x, along_y, along_z, estimate, correction
):
    part, total_rows, lanes = recorded.shape
    flat = (part * total_rows, lanes)
    joined = jnp.sqrt(jnp.sqrt(product[...] * received[...]))
    cells = (recorded[...] * joined).reshape(flat)
    edges = [ref[...].reshape(flat) for ref in (along_x, along_y, along_z)]
    for _ in range(SWEEPS):
        cells = swept(cells, *edges, total_rows, depth_cells)
    estimate[...] = cells.reshape(estimate.shape)
    correction[...] = corrected(recorded[...].reshape(flat), cells, band_in[...]).reshape(
        correction.shape
    )


def windows_kernel(tiles, depth_cells, own, other, kept, sent, product):
    product[...] = own[...] * exchanged(other[...], depth_cells)
    slab = product.shape[1] // tiles
    slot = own_slot(tiles)
    kept[...] = window(product, slot, tiles, slab, SWEEPS)
    sent[...] = window(product, tiles - 1 - slot, tiles, slab, SWEEPS)


def near_kernel(tiles, estimate, along_x, along_y, along_z, *outs):
    slot = own_slot(tiles)
    slab = estimate.shape[1] // tiles
    for ref, out in zip((estimate, along_x, along_y, along_z), outs):
        out[...] = window(ref, slot, tiles, slab, SWEEPS)


def last_kernel(groups, depth_cells, estimate, kept, received, along_x, along_y, along_z, out, held):
    part, extent, lanes = estimate.shape
    slab = extent - 2 * SWEEPS
    flat = (part * extent, lanes)
    joined = jnp.sqrt(jnp.sqrt(kept[...] * received[...]))
    cells = (estimate[...] * joined).reshape(flat)
    edges = [ref[...].reshape(flat) for ref in (along_x, along_y, along_z)]
    for _ in range(SWEEPS):
        cells = swept(cells, *edges, extent, depth_cells)
    cells = cells.reshape(part, extent, lanes)[:, SWEEPS : SWEEPS + slab]
    cells = cells.reshape(part * slab, lanes)
    cells = jnp.take_along_axis(cells, lane_order(cells.shape, depth_cells), axis=1)
    cells = cells.reshape(part, slab, lanes)
    cells = jnp.concatenate(
        [cells[:, :, g * depth_cells : (g + 1) * depth_cells] for g in range(groups)], axis=0
    )
    held[...] = jnp.swapaxes(cells, 0, 1)
    turn = rows_reversed()
    for i in range(slab):
        out[0, i] = held[jnp.where(turn, slab - 1 - i, i)]


def whole_views(data, labels, kernel, offsets):
    tiles = lax.axis_size("tile")
    _, slab, rows, depth_cells = data.shape
    groups = LANES // depth_cells
    part = rows // groups
    total_rows = slab * tiles
    extent = slab + 2 * SWEEPS
    f32 = jnp.float32
    block = (part, slab, LANES)
    view = (part, total_rows, LANES)
    near = (part, extent, LANES)
    vmem = pl.BlockSpec(memory_space=pltpu.VMEM)

    def call(body, outs, scratch, *args):
        shapes = tuple(jax.ShapeDtypeStruct(s, d) for s, d in outs)
        return pl.pallas_call(
            body,
            out_shape=shapes,
            in_specs=[vmem] * len(args),
            out_specs=tuple(vmem for _ in shapes),
            scratch_shapes=scratch,
            compiler_params=pltpu.CompilerParams(vmem_limit_bytes=32 << 20),
        )(*args)

    def gathered(own):
        return [own] + [
            lax.ppermute(own, "tile", [(i, i ^ k) for i in range(tiles)]) for k in range(1, tiles)
        ]

    def swap(cells, bit):
        return lax.ppermute(cells, "view", [(i, i ^ bit) for i in range(VIEWS)])

    packed, packed_labels = call(
        functools.partial(pack_kernel, groups),
        [(block, f32), (block, jnp.int32)],
        [pltpu.VMEM(data.shape[1:], f32), pltpu.VMEM(data.shape[1:], jnp.int32)],
        data,
        labels,
    )
    (matrix,) = call(band_kernel, [((LANES, LANES), f32)], [], kernel, offsets)
    blocks = gathered(packed)
    label_blocks = gathered(packed_labels)
    recorded, correction = call(
        functools.partial(first_kernel, tiles), [(view, f32)] * 2, [], matrix, *blocks
    )
    other = swap(correction, 1)
    (product,) = call(
        functools.partial(product_kernel, depth_cells), [(view, f32)], [], correction, other
    )
    edges = call(
        functools.partial(edges_kernel, tiles, depth_cells),
        [(view, f32)] * 3,
        [pltpu.VMEM(view, jnp.int32)],
        *label_blocks,
    )
    received = swap(product, 2)
    estimate, correction = call(
        functools.partial(second_kernel, depth_cells),
        [(view, f32)] * 2,
        [],
        matrix,
        recorded,
        product,
        received,
        *edges,
    )
    other = swap(correction, 1)
    near_cells = call(
        functools.partial(near_kernel, tiles), [(near, f32)] * 4, [], estimate, *edges
    )
    kept, sent = call(
        functools.partial(windows_kernel, tiles, depth_cells),
        [(near, f32)] * 2,
        [pltpu.VMEM(view, f32)],
        correction,
        other,
    )
    received = swap(sent, 2)
    (out,) = call(
        functools.partial(last_kernel, groups, depth_cells),
        [(data.shape, f32)],
        [pltpu.VMEM(data.shape[1:], f32)],
        near_cells[0],
        kept,
        received,
        *near_cells[1:],
    )
    return out


def fits_whole(shape):
    _, slab, rows, depth_cells = shape
    tiles = lax.axis_size("tile")
    return (
        lax.axis_size("view") == VIEWS
        and ITERS == 2
        and slab % ROWS == 0
        and slab >= SWEEPS
        and slab * tiles == depth_cells
        and tiles & (tiles - 1) == 0
        and LANES % depth_cells == 0
        and rows % (LANES // depth_cells) ** 2 == 0
        and (2 * SWEEPS) % ROWS == 0
    )


def on_device(data, labels, kernel, offsets):
    form = whole_views if fits_whole(data.shape) else by_slabs
    return form(data, labels, kernel, offsets)


def solution(mesh):
    placed = (
        P(("parts", "view"), "tile", None, None),
        P(("parts", "view"), "tile", None, None),
        P("view", None, None),
        P("view", None),
    )
    return jax.shard_map(
        on_device,
        mesh=mesh,
        in_specs=placed,
        out_specs=P(("parts", "view"), "tile", None, None),
        check_vma=False,
    )
```

```python
import functools

import jax
import jax.experimental.pallas as pl
import jax.experimental.pallas.tpu as pltpu
import jax.numpy as jnp
from jax import lax
from jax.sharding import PartitionSpec as P

ITERS = 2
SWEEPS = 4

WEAK = 0.2
TAU = 0.15

LANES = 128
ROWS = 8
VIEWS = 4


def extended(cells, sides, width):
    for axis, dim in sides:
        count = lax.axis_size(axis)
        ends = count - 1
        head = lax.slice_in_dim(cells, 0, width, axis=dim)
        tail = lax.slice_in_dim(cells, cells.shape[dim] - width, cells.shape[dim], axis=dim)
        cells = jnp.concatenate(
            [
                lax.ppermute(tail, axis, [(i, (i + 1) % count) for i in range(ends)]),
                cells,
                lax.ppermute(head, axis, [((i + 1) % count, i) for i in range(ends)]),
            ],
            axis=dim,
        )
    return cells


def swapped(block, axis, stride):
    count = lax.axis_size(axis)
    route = []
    for low in range(count):
        high = low | 1 << stride
        if high != low and high < count:
            route += [(low, high), (high, low)]
    return lax.ppermute(block, axis, route)


def band(kernel, offsets):
    depth_cells = kernel.shape[0]
    taps = jnp.arange(kernel.shape[1], dtype=jnp.int32) - 4
    depth = jnp.arange(depth_cells, dtype=jnp.int32)
    index = jnp.clip(depth[:, None] + taps[None, :] + offsets[:, None], 0, depth_cells - 1)
    weight = kernel / jnp.sum(kernel, axis=1, keepdims=True)
    return (index, weight)


def axis_term(field, region, axis):
    count = field.shape[axis]
    upper = lax.slice_in_dim(field, 1, count, axis=axis)
    lower = lax.slice_in_dim(field, 0, count - 1, axis=axis)
    same = jnp.where(
        lax.slice_in_dim(region, 1, count, axis=axis)
        == lax.slice_in_dim(region, 0, count - 1, axis=axis),
        1.0,
        WEAK,
    )
    flux = same * (upper - lower)
    after = [(0, 0)] * 3
    before = [(0, 0)] * 3
    after[axis] = (0, 1)
    before[axis] = (1, 0)
    return jnp.pad(flux, after) - jnp.pad(flux, before)


def sweep_rows(field, region, first_row, total_rows):
    extent = field.shape[0]
    global_rows = first_row + jnp.arange(extent, dtype=jnp.int32)
    inside = ((global_rows >= 0) & (global_rows < total_rows)).astype(field.dtype)[:, None, None]
    same = jnp.where(region[1:] == region[:-1], 1.0, WEAK) * inside[1:] * inside[:-1]
    flux = same * (field[1:] - field[:-1])
    inner = field[1:-1]
    inner_labels = region[1:-1]
    total = (
        flux[1:] - flux[:-1] + axis_term(inner, inner_labels, 1) + axis_term(inner, inner_labels, 2)
    )
    return inner + TAU * total


def regroup(received, tiles):
    slab, rows, depth_cells = received.shape
    blocks = received.reshape(slab, rows, tiles, depth_cells // tiles)
    return blocks.transpose(3, 1, 2, 0).reshape(depth_cells // tiles, rows, depth_cells)


def by_slabs(data, labels, kernel, offsets):
    recorded = data[0]
    region = labels[0]
    index, weight = band(kernel[0], offsets[0])
    tiles = lax.axis_size("tile")
    slab, rows, depth_cells = recorded.shape
    total_rows = slab * tiles
    start = lax.axis_index("tile") * slab
    parity = lax.axis_index("view") % 2
    columns = jnp.arange(depth_cells, dtype=jnp.int32)
    matrix = jnp.sum(weight[:, :, None] * (index[:, :, None] == columns[None, None, :]), axis=1)
    label_ext = extended(region, (("tile", 0),), SWEEPS)
    views = lax.axis_size("view")
    half_turn = [
        (v * tiles + t, (v + 2) % views * tiles + tiles - 1 - t)
        for v in range(views)
        for t in range(tiles)
    ]
    current = recorded
    for step in range(ITERS):
        forward_flat = jnp.dot(
            current.reshape(-1, depth_cells), matrix.T, precision=lax.Precision.HIGHEST
        )
        field = recorded / forward_flat.reshape(current.shape)
        flat = jnp.dot(field.reshape(-1, depth_cells), matrix, precision=lax.Precision.HIGHEST)
        correction = flat.reshape(field.shape)
        turned = jnp.flip(lax.ppermute(correction, ("view", "tile"), half_turn), (0, 2))
        paired = jnp.sqrt(correction * turned)
        outgoing = jnp.where(parity == 0, jnp.flip(paired, 2), paired)
        rotated = regroup(
            lax.all_to_all(outgoing, "tile", split_axis=2, concat_axis=2, tiled=True), tiles
        )
        rotated = jnp.where(parity == 1, jnp.flip(rotated, 2), rotated)
        partner = swapped(rotated, "view", 0)
        current = current * jnp.sqrt(paired * partner)
        widened = extended(current, (("tile", 0),), SWEEPS)
        for sweep in range(SWEEPS):
            extent = widened.shape[0]
            widened = sweep_rows(
                widened,
                label_ext[sweep : sweep + extent],
                start - SWEEPS + sweep,
                total_rows,
            )
        current = widened
    return current[None]


def rows_reversed():
    v = lax.axis_index("view")
    return lax.rem(v + 1, VIEWS) >= 2


def depth_reversed():
    return lax.axis_index("view") >= 2


def own_slot(tiles):
    t = lax.axis_index("tile")
    return jnp.where(rows_reversed(), tiles - 1 - t, t)


def lane_order(shape, depth_cells):
    lane = lax.broadcasted_iota(jnp.int32, shape, 1)
    base = lane // depth_cells * depth_cells
    return jnp.where(depth_reversed(), base + (base + depth_cells - 1 - lane), lane)


def pack_one(source, held, target, groups):
    slab, rows, depth_cells = held.shape
    turn = rows_reversed()
    for i in range(slab):
        held[i] = source[0, jnp.where(turn, slab - 1 - i, i)]
    part = rows // groups
    cells = jnp.swapaxes(held[...], 0, 1)
    cells = jnp.concatenate([cells[g * part : (g + 1) * part] for g in range(groups)], axis=2)
    flat = cells.reshape(part * slab, groups * depth_cells)
    order = lane_order(flat.shape, depth_cells)
    flat = jnp.take_along_axis(flat, order, axis=1)
    target[...] = flat.reshape(target.shape).astype(target.dtype)


def pack_kernel(groups, data, labels, data_out, both_out, held, held_labels):
    pack_one(data, held, data_out, groups)
    part = data_out.shape[0]
    both_out[:part] = data_out[...]
    pack_one(labels, held_labels, both_out.at[part:], groups)


def split(cells):
    high = cells.astype(jnp.bfloat16)
    return high, (cells - high.astype(jnp.float32)).astype(jnp.bfloat16)


def band_kernel(kernel, offsets, blur_out, adjoint_out):
    depth_cells, taps = kernel.shape[1:]
    span = blur_out.shape[0] // 2
    turn = depth_reversed()
    row = lax.broadcasted_iota(jnp.int32, (depth_cells, depth_cells), 0)
    col = lax.broadcasted_iota(jnp.int32, (depth_cells, depth_cells), 1)
    pick = col == jnp.where(turn, depth_cells - 1 - row, row)
    shift = jnp.sum(
        jnp.where(pick, jnp.broadcast_to(offsets[...], pick.shape), 0), axis=1, keepdims=True
    )
    depth = row[:, :1]
    depth = jnp.where(turn, depth_cells - 1 - depth, depth)
    taps_by_row = jnp.dot(
        pick.astype(jnp.float32),
        kernel[0],
        precision=lax.Precision.HIGHEST,
        preferred_element_type=jnp.float32,
    )
    weight = taps_by_row / jnp.sum(taps_by_row, axis=1, keepdims=True)
    lane = lax.broadcasted_iota(jnp.int32, (depth_cells, span), 1)
    within = lax.rem(lane, depth_cells)
    within = jnp.where(turn, depth_cells - 1 - within, within)
    total = jnp.zeros((depth_cells, span), jnp.float32)
    for k in range(taps):
        index = jnp.clip(depth + (k - 4) + shift, 0, depth_cells - 1)
        total = total + jnp.where(index == within, weight[:, k : k + 1], 0.0)
    matrix = jnp.concatenate(
        [jnp.where(lane // depth_cells == g, total, 0.0) for g in range(span // depth_cells)], axis=0
    )
    for cells, out in ((matrix.T, blur_out), (matrix, adjoint_out)):
        high, low = split(cells)
        for half in range(2):
            out[half * span : (half + 1) * span, :span] = high
            out[half * span : (half + 1) * span, span:] = low


def banded(cells, band):
    high, low = split(cells)
    both = jnp.dot(
        jnp.concatenate([high, low], axis=1), band[...], preferred_element_type=jnp.float32
    )
    lanes = cells.shape[1]
    return both[:, :lanes] + both[:, lanes:]


def corrected(recorded, estimate, blur_band, adjoint_band):
    return banded(recorded / banded(estimate, blur_band), adjoint_band)


def first_correction(block, blur_band, adjoint_band):
    flat = block.reshape(-1, block.shape[-1])
    return corrected(flat, flat, blur_band, adjoint_band).reshape(block.shape)


def place(target, slot, block):
    slab = block.shape[1]
    target[:, pl.ds(pl.multiple_of(slot * slab, slab), slab), :] = block


def block_kernel(blur_band, adjoint_band, block, correction):
    correction[...] = first_correction(block[...], blur_band, adjoint_band)


def beside_kernel(blur_band, adjoint_band, own_both, both, correction, labels_out):
    part = both.shape[0] // 2
    correction[...] = first_correction(both[:part], blur_band, adjoint_band)
    labels_out[:part] = own_both[part:]
    labels_out[part:] = both[part:]


def last_block_kernel(tiles, k, others, blur_band, adjoint_band, block, *refs):
    correction = refs[-1]
    slot = own_slot(tiles)
    for j, ref in zip(others, refs):
        place(correction, slot ^ j, ref[...])
    place(correction, slot ^ k, first_correction(block[...], blur_band, adjoint_band))


def recorded_kernel(tiles, own, both, *refs):
    far, recorded = refs[:-1], refs[-1]
    slot = own_slot(tiles)
    place(recorded, slot, own[...])
    place(recorded, slot ^ 1, both[: own.shape[0]])
    for k, ref in enumerate(far):
        place(recorded, slot ^ (k + 2), ref[...])


def edges_kernel(tiles, depth_cells, near, far, along_x, along_y, along_z, whole):
    slot = own_slot(tiles)
    slab, lanes = near.shape[1:]
    part = near.shape[0] // 2
    for k in range(tiles):
        source = (near, far)[k // 2]
        place(whole, slot ^ k, source[k % 2 * part : (k % 2 + 1) * part])
    total_rows = tiles * slab
    region = whole[...].reshape(part * total_rows, lanes)
    row = lax.broadcasted_iota(jnp.int32, region.shape, 0)
    lane = lax.broadcasted_iota(jnp.int32, region.shape, 1)

    def weighted(upper, inside, target):
        same = jnp.where(upper == region, TAU, TAU * WEAK)
        target[...] = jnp.where(inside, same, 0.0).reshape(target.shape)

    weighted(up_rows(region), lax.rem(row, total_rows) != total_rows - 1, along_x)
    weighted(
        up_second(region, total_rows, depth_cells),
        (row < (part - 1) * total_rows) | (lane < lanes - depth_cells),
        along_y,
    )
    weighted(up_depth(region), lax.rem(lane, depth_cells) != depth_cells - 1, along_z)


def up_rows(cells):
    return pltpu.roll(cells, cells.shape[0] - 1, 0)


def up_depth(cells):
    return pltpu.roll(cells, cells.shape[1] - 1, 1)


def up_second(cells, total_rows, depth_cells):
    first = pltpu.roll(cells[:total_rows], cells.shape[1] - depth_cells, 1)
    return jnp.concatenate([cells[total_rows:], first], axis=0)


def down_second(cells, total_rows, depth_cells):
    last = pltpu.roll(cells[-total_rows:], depth_cells, 1)
    return jnp.concatenate([last, cells[:-total_rows]], axis=0)


def swept(cells, along_x, along_y, along_z, total_rows, depth_cells):
    flux_x = along_x * (up_rows(cells) - cells)
    flux_y = along_y * (up_second(cells, total_rows, depth_cells) - cells)
    flux_z = along_z * (up_depth(cells) - cells)
    return (
        cells
        + (flux_x - pltpu.roll(flux_x, 1, 0))
        + (flux_y - down_second(flux_y, total_rows, depth_cells))
        + (flux_z - pltpu.roll(flux_z, 1, 1))
    )


def exchanged(cells, depth_cells):
    part, rows, lanes = cells.shape
    groups = lanes // depth_cells
    lane_group = lax.broadcasted_iota(jnp.int32, (rows, lanes), 1) // depth_cells
    out = []
    for first in range(0, part, groups):
        turned = cells[first : first + groups].reshape(groups * rows, lanes).T
        for a in range(groups):
            plane = None
            for b in range(groups):
                piece = turned[b * rows : (b + 1) * rows]
                moved = (b - a) % groups * depth_cells
                if moved:
                    piece = pltpu.roll(piece, moved, 1)
                plane = piece if plane is None else jnp.where(lane_group == b, piece, plane)
            out.append(plane)
    return jnp.stack(out)


def product_kernel(depth_cells, own, other, product):
    product[...] = own[...] * exchanged(other[...], depth_cells)


def window(ref, slot, tiles, slab, margin):
    parts = []
    for step in (-1, 0, 1):
        at = lax.rem(slot + step + tiles, tiles) * slab
        parts.append(ref[:, pl.ds(pl.multiple_of(at, slab), slab), :])
    return jnp.concatenate(parts, axis=1)[:, slab - margin : 2 * slab + margin, :]


def second_kernel(
    depth_cells,
    blur_band,
    adjoint_band,
    recorded,
    product,
    received,
    along_x,
    along_y,
    along_z,
    estimate,
    correction,
):
    part, total_rows, lanes = recorded.shape
    flat = (part * total_rows, lanes)
    joined = lax.rsqrt(lax.rsqrt(product[...] * received[...]))
    cells = (recorded[...] * joined).reshape(flat)
    edges = [ref[...].reshape(flat) for ref in (along_x, along_y, along_z)]
    for _ in range(SWEEPS):
        cells = swept(cells, *edges, total_rows, depth_cells)
    estimate[...] = cells.reshape(estimate.shape)
    correction[...] = corrected(
        recorded[...].reshape(flat), cells, blur_band, adjoint_band
    ).reshape(correction.shape)


def windows_kernel(tiles, depth_cells, own, other, kept, sent, product):
    product[...] = own[...] * exchanged(other[...], depth_cells)
    slab = product.shape[1] // tiles
    slot = own_slot(tiles)
    kept[...] = window(product, slot, tiles, slab, SWEEPS)
    sent[...] = window(product, tiles - 1 - slot, tiles, slab, SWEEPS)


def near_kernel(tiles, estimate, along_x, along_y, along_z, *outs):
    slot = own_slot(tiles)
    slab = estimate.shape[1] // tiles
    for ref, out in zip((estimate, along_x, along_y, along_z), outs):
        out[...] = window(ref, slot, tiles, slab, SWEEPS)


def last_kernel(groups, depth_cells, estimate, kept, received, along_x, along_y, along_z, out, held):
    part, extent, lanes = estimate.shape
    slab = extent - 2 * SWEEPS
    flat = (part * extent, lanes)
    joined = lax.rsqrt(lax.rsqrt(kept[...] * received[...]))
    cells = (estimate[...] * joined).reshape(flat)
    edges = [ref[...].reshape(flat) for ref in (along_x, along_y, along_z)]
    for _ in range(SWEEPS):
        cells = swept(cells, *edges, extent, depth_cells)
    cells = cells.reshape(part, extent, lanes)[:, SWEEPS : SWEEPS + slab]
    cells = cells.reshape(part * slab, lanes)
    cells = jnp.take_along_axis(cells, lane_order(cells.shape, depth_cells), axis=1)
    cells = cells.reshape(part, slab, lanes)
    cells = jnp.concatenate(
        [cells[:, :, g * depth_cells : (g + 1) * depth_cells] for g in range(groups)], axis=0
    )
    held[...] = jnp.swapaxes(cells, 0, 1)
    turn = rows_reversed()
    for i in range(slab):
        out[0, i] = held[jnp.where(turn, slab - 1 - i, i)]


def whole_views(data, labels, kernel, offsets):
    tiles = lax.axis_size("tile")
    _, slab, rows, depth_cells = data.shape
    groups = LANES // depth_cells
    part = rows // groups
    total_rows = slab * tiles
    extent = slab + 2 * SWEEPS
    f32 = jnp.float32
    block = (part, slab, LANES)
    view = (part, total_rows, LANES)
    near = (part, extent, LANES)
    vmem = pl.BlockSpec(memory_space=pltpu.VMEM)

    def call(body, outs, scratch, *args):
        shapes = tuple(jax.ShapeDtypeStruct(s, d) for s, d in outs)
        return pl.pallas_call(
            body,
            out_shape=shapes,
            in_specs=[vmem] * len(args),
            out_specs=tuple(vmem for _ in shapes),
            scratch_shapes=scratch,
            compiler_params=pltpu.CompilerParams(vmem_limit_bytes=32 << 20),
        )(*args)

    def across(cells, k):
        return lax.ppermute(cells, "tile", [(i, i ^ k) for i in range(tiles)])

    def swap(cells, bit):
        return lax.ppermute(cells, "view", [(i, i ^ bit) for i in range(VIEWS)])

    packed, both = call(
        functools.partial(pack_kernel, groups),
        [(block, f32), ((2 * part,) + block[1:], f32)],
        [pltpu.VMEM(data.shape[1:], f32), pltpu.VMEM(data.shape[1:], jnp.int32)],
        data,
        labels,
    )
    bands = call(band_kernel, [((2 * LANES, 2 * LANES), jnp.bfloat16)] * 2, [], kernel, offsets)
    blocks = {k: across(packed, k) for k in range(tiles - 1, 1, -1)}
    beside = across(both, 1)
    (made_own,) = call(block_kernel, [(block, f32)], [], *bands, packed)
    made_beside, near_labels = call(
        beside_kernel, [(block, f32), ((2 * part,) + block[1:], f32)], [], *bands, both, beside
    )
    (made_far,) = call(block_kernel, [(block, f32)], [], *bands, blocks[3])
    (correction,) = call(
        functools.partial(last_block_kernel, tiles, 2, (0, 1, 3)),
        [(view, f32)],
        [],
        *bands,
        blocks[2],
        made_own,
        made_beside,
        made_far,
    )
    (recorded,) = call(
        functools.partial(recorded_kernel, tiles),
        [(view, f32)],
        [],
        packed,
        beside,
        blocks[2],
        blocks[3],
    )
    far_labels = across(near_labels, 2)
    other = swap(correction, 1)
    (product,) = call(
        functools.partial(product_kernel, depth_cells), [(view, f32)], [], correction, other
    )
    edges = call(
        functools.partial(edges_kernel, tiles, depth_cells),
        [(view, f32)] * 3,
        [pltpu.VMEM(view, f32)],
        near_labels,
        far_labels,
    )
    received = swap(product, 2)
    estimate, correction = call(
        functools.partial(second_kernel, depth_cells),
        [(view, f32)] * 2,
        [],
        *bands,
        recorded,
        product,
        received,
        *edges,
    )
    other = swap(correction, 1)
    near_cells = call(
        functools.partial(near_kernel, tiles), [(near, f32)] * 4, [], estimate, *edges
    )
    kept, sent = call(
        functools.partial(windows_kernel, tiles, depth_cells),
        [(near, f32)] * 2,
        [pltpu.VMEM(view, f32)],
        correction,
        other,
    )
    received = swap(sent, 2)
    (out,) = call(
        functools.partial(last_kernel, groups, depth_cells),
        [(data.shape, f32)],
        [pltpu.VMEM(data.shape[1:], f32)],
        near_cells[0],
        kept,
        received,
        *near_cells[1:],
    )
    return out


def fits_whole(shape):
    _, slab, rows, depth_cells = shape
    tiles = lax.axis_size("tile")
    return (
        lax.axis_size("view") == VIEWS
        and ITERS == 2
        and slab % ROWS == 0
        and slab >= SWEEPS
        and slab * tiles == depth_cells
        and tiles == 4
        and LANES % depth_cells == 0
        and rows % (LANES // depth_cells) ** 2 == 0
        and (2 * SWEEPS) % ROWS == 0
    )


def on_device(data, labels, kernel, offsets):
    form = whole_views if fits_whole(data.shape) else by_slabs
    return form(data, labels, kernel, offsets)


def solution(mesh):
    placed = (
        P(("parts", "view"), "tile", None, None),
        P(("parts", "view"), "tile", None, None),
        P("view", None, None),
        P("view", None),
    )
    return jax.shard_map(
        on_device,
        mesh=mesh,
        in_specs=placed,
        out_specs=P(("parts", "view"), "tile", None, None),
        check_vma=False,
    )
```

```python
import functools

import jax
import jax.experimental.pallas as pl
import jax.experimental.pallas.tpu as pltpu
import jax.numpy as jnp
from jax import lax
from jax.sharding import PartitionSpec as P

ITERS = 2
SWEEPS = 4

WEAK = 0.2
TAU = 0.15

LANES = 128
ROWS = 8
VIEWS = 4

LABELS_WITH = 3
LABELS_BY = 1


def extended(cells, sides, width):
    for axis, dim in sides:
        count = lax.axis_size(axis)
        ends = count - 1
        head = lax.slice_in_dim(cells, 0, width, axis=dim)
        tail = lax.slice_in_dim(cells, cells.shape[dim] - width, cells.shape[dim], axis=dim)
        cells = jnp.concatenate(
            [
                lax.ppermute(tail, axis, [(i, (i + 1) % count) for i in range(ends)]),
                cells,
                lax.ppermute(head, axis, [((i + 1) % count, i) for i in range(ends)]),
            ],
            axis=dim,
        )
    return cells


def swapped(block, axis, stride):
    count = lax.axis_size(axis)
    route = []
    for low in range(count):
        high = low | 1 << stride
        if high != low and high < count:
            route += [(low, high), (high, low)]
    return lax.ppermute(block, axis, route)


def band(kernel, offsets):
    depth_cells = kernel.shape[0]
    taps = jnp.arange(kernel.shape[1], dtype=jnp.int32) - 4
    depth = jnp.arange(depth_cells, dtype=jnp.int32)
    index = jnp.clip(depth[:, None] + taps[None, :] + offsets[:, None], 0, depth_cells - 1)
    weight = kernel / jnp.sum(kernel, axis=1, keepdims=True)
    return (index, weight)


def axis_term(field, region, axis):
    count = field.shape[axis]
    upper = lax.slice_in_dim(field, 1, count, axis=axis)
    lower = lax.slice_in_dim(field, 0, count - 1, axis=axis)
    same = jnp.where(
        lax.slice_in_dim(region, 1, count, axis=axis)
        == lax.slice_in_dim(region, 0, count - 1, axis=axis),
        1.0,
        WEAK,
    )
    flux = same * (upper - lower)
    after = [(0, 0)] * 3
    before = [(0, 0)] * 3
    after[axis] = (0, 1)
    before[axis] = (1, 0)
    return jnp.pad(flux, after) - jnp.pad(flux, before)


def sweep_rows(field, region, first_row, total_rows):
    extent = field.shape[0]
    global_rows = first_row + jnp.arange(extent, dtype=jnp.int32)
    inside = ((global_rows >= 0) & (global_rows < total_rows)).astype(field.dtype)[:, None, None]
    same = jnp.where(region[1:] == region[:-1], 1.0, WEAK) * inside[1:] * inside[:-1]
    flux = same * (field[1:] - field[:-1])
    inner = field[1:-1]
    inner_labels = region[1:-1]
    total = (
        flux[1:] - flux[:-1] + axis_term(inner, inner_labels, 1) + axis_term(inner, inner_labels, 2)
    )
    return inner + TAU * total


def regroup(received, tiles):
    slab, rows, depth_cells = received.shape
    blocks = received.reshape(slab, rows, tiles, depth_cells // tiles)
    return blocks.transpose(3, 1, 2, 0).reshape(depth_cells // tiles, rows, depth_cells)


def by_slabs(data, labels, kernel, offsets):
    recorded = data[0]
    region = labels[0]
    index, weight = band(kernel[0], offsets[0])
    tiles = lax.axis_size("tile")
    slab, rows, depth_cells = recorded.shape
    total_rows = slab * tiles
    start = lax.axis_index("tile") * slab
    parity = lax.axis_index("view") % 2
    columns = jnp.arange(depth_cells, dtype=jnp.int32)
    matrix = jnp.sum(weight[:, :, None] * (index[:, :, None] == columns[None, None, :]), axis=1)
    label_ext = extended(region, (("tile", 0),), SWEEPS)
    views = lax.axis_size("view")
    half_turn = [
        (v * tiles + t, (v + 2) % views * tiles + tiles - 1 - t)
        for v in range(views)
        for t in range(tiles)
    ]
    current = recorded
    for step in range(ITERS):
        forward_flat = jnp.dot(
            current.reshape(-1, depth_cells), matrix.T, precision=lax.Precision.HIGHEST
        )
        field = recorded / forward_flat.reshape(current.shape)
        flat = jnp.dot(field.reshape(-1, depth_cells), matrix, precision=lax.Precision.HIGHEST)
        correction = flat.reshape(field.shape)
        turned = jnp.flip(lax.ppermute(correction, ("view", "tile"), half_turn), (0, 2))
        paired = jnp.sqrt(correction * turned)
        outgoing = jnp.where(parity == 0, jnp.flip(paired, 2), paired)
        rotated = regroup(
            lax.all_to_all(outgoing, "tile", split_axis=2, concat_axis=2, tiled=True), tiles
        )
        rotated = jnp.where(parity == 1, jnp.flip(rotated, 2), rotated)
        partner = swapped(rotated, "view", 0)
        current = current * jnp.sqrt(paired * partner)
        widened = extended(current, (("tile", 0),), SWEEPS)
        for sweep in range(SWEEPS):
            extent = widened.shape[0]
            widened = sweep_rows(
                widened,
                label_ext[sweep : sweep + extent],
                start - SWEEPS + sweep,
                total_rows,
            )
        current = widened
    return current[None]


def rows_reversed():
    v = lax.axis_index("view")
    return lax.rem(v + 1, VIEWS) >= 2


def depth_reversed():
    return lax.axis_index("view") >= 2


def own_slot(tiles):
    t = lax.axis_index("tile")
    return jnp.where(rows_reversed(), tiles - 1 - t, t)


def lane_order(shape, depth_cells):
    lane = lax.broadcasted_iota(jnp.int32, shape, 1)
    base = lane // depth_cells * depth_cells
    return jnp.where(depth_reversed(), base + (base + depth_cells - 1 - lane), lane)


def pack_one(source, held, target, groups):
    slab, rows, depth_cells = held.shape
    turn = rows_reversed()
    for i in range(slab):
        held[i] = source[0, jnp.where(turn, slab - 1 - i, i)]
    part = rows // groups
    cells = jnp.swapaxes(held[...], 0, 1)
    cells = jnp.concatenate([cells[g * part : (g + 1) * part] for g in range(groups)], axis=2)
    flat = cells.reshape(part * slab, groups * depth_cells)
    order = lane_order(flat.shape, depth_cells)
    flat = jnp.take_along_axis(flat, order, axis=1)
    target[...] = flat.reshape(target.shape).astype(target.dtype)


def pack_kernel(groups, data, labels, data_out, both_out, held, held_labels):
    pack_one(data, held, data_out, groups)
    part = data_out.shape[0]
    both_out[:part] = data_out[...]
    pack_one(labels, held_labels, both_out.at[part:], groups)


def split(cells):
    high = cells.astype(jnp.bfloat16)
    return high, (cells - high.astype(jnp.float32)).astype(jnp.bfloat16)


def band_kernel(kernel, offsets, blur_out, adjoint_out):
    depth_cells, taps = kernel.shape[1:]
    span = blur_out.shape[0] // 2
    turn = depth_reversed()
    row = lax.broadcasted_iota(jnp.int32, (depth_cells, depth_cells), 0)
    col = lax.broadcasted_iota(jnp.int32, (depth_cells, depth_cells), 1)
    pick = col == jnp.where(turn, depth_cells - 1 - row, row)
    shift = jnp.sum(
        jnp.where(pick, jnp.broadcast_to(offsets[...], pick.shape), 0), axis=1, keepdims=True
    )
    depth = row[:, :1]
    depth = jnp.where(turn, depth_cells - 1 - depth, depth)
    taps_by_row = jnp.dot(
        pick.astype(jnp.float32),
        kernel[0],
        precision=lax.Precision.HIGHEST,
        preferred_element_type=jnp.float32,
    )
    weight = taps_by_row / jnp.sum(taps_by_row, axis=1, keepdims=True)
    lane = lax.broadcasted_iota(jnp.int32, (depth_cells, span), 1)
    within = lax.rem(lane, depth_cells)
    within = jnp.where(turn, depth_cells - 1 - within, within)
    total = jnp.zeros((depth_cells, span), jnp.float32)
    for k in range(taps):
        index = jnp.clip(depth + (k - 4) + shift, 0, depth_cells - 1)
        total = total + jnp.where(index == within, weight[:, k : k + 1], 0.0)
    matrix = jnp.concatenate(
        [jnp.where(lane // depth_cells == g, total, 0.0) for g in range(span // depth_cells)], axis=0
    )
    for cells, out in ((matrix.T, blur_out), (matrix, adjoint_out)):
        high, low = split(cells)
        for half in range(2):
            out[half * span : (half + 1) * span, :span] = high
            out[half * span : (half + 1) * span, span:] = low


def banded(cells, band):
    high, low = split(cells)
    both = jnp.dot(
        jnp.concatenate([high, low], axis=1), band[...], preferred_element_type=jnp.float32
    )
    lanes = cells.shape[1]
    return both[:, :lanes] + both[:, lanes:]


def corrected(recorded, estimate, blur_band, adjoint_band):
    return banded(recorded / banded(estimate, blur_band), adjoint_band)


def first_correction(block, blur_band, adjoint_band):
    flat = block.reshape(-1, block.shape[-1])
    return corrected(flat, flat, blur_band, adjoint_band).reshape(block.shape)


def place(target, slot, block):
    slab = block.shape[1]
    target[:, pl.ds(pl.multiple_of(slot * slab, slab), slab), :] = block


def blocks_kernel(blur_band, adjoint_band, *refs):
    blocks, correction = refs[:-1], refs[-1]
    part = correction.shape[0] // len(blocks)
    cells = jnp.concatenate([block[:part] for block in blocks], axis=0)
    correction[...] = first_correction(cells, blur_band, adjoint_band)


def relay_kernel(own_both, both, labels_out):
    part = both.shape[0] // 2
    labels_out[:part] = own_both[part:]
    labels_out[part:] = both[part:]


def pair_kernel(tiles, *refs):
    own, far, products = refs[:2], refs[2:4], refs[4:]
    pair = own[0].shape[0]
    part = pair // 2
    slot = own_slot(tiles)
    for k in range(tiles):
        mine, theirs = k * part, (tiles - 1 - k) * part
        near = own[mine // pair][mine % pair : mine % pair + part]
        cells = near * far[theirs // pair][theirs % pair : theirs % pair + part]
        for i, product in enumerate(products):
            size = product.shape[0]
            place(product, slot ^ k, cells[i * size : (i + 1) * size])


def recorded_kernel(tiles, *refs):
    blocks, recorded = refs[:-1], refs[-1]
    slot = own_slot(tiles)
    for k, ref in enumerate(blocks):
        place(recorded, slot ^ k, ref[: recorded.shape[0]])


def edges_kernel(tiles, depth_cells, near, far, along_x, along_y, along_z, whole):
    slot = own_slot(tiles)
    slab, lanes = near.shape[1:]
    part = near.shape[0] // 2
    for k in range(tiles):
        if k in (0, LABELS_WITH):
            cells = near[part:] if k else near[:part]
        else:
            cells = far[:part] if k == LABELS_BY else far[part:]
        place(whole, slot ^ k, cells)
    total_rows = tiles * slab
    region = whole[...].reshape(part * total_rows, lanes)
    row = lax.broadcasted_iota(jnp.int32, region.shape, 0)
    lane = lax.broadcasted_iota(jnp.int32, region.shape, 1)

    def weighted(upper, inside, target):
        same = jnp.where(upper == region, TAU, TAU * WEAK)
        target[...] = jnp.where(inside, same, 0.0).reshape(target.shape)

    weighted(up_rows(region), lax.rem(row, total_rows) != total_rows - 1, along_x)
    weighted(
        up_second(region, total_rows, depth_cells),
        (row < (part - 1) * total_rows) | (lane < lanes - depth_cells),
        along_y,
    )
    weighted(up_depth(region), lax.rem(lane, depth_cells) != depth_cells - 1, along_z)


def up_rows(cells):
    return pltpu.roll(cells, cells.shape[0] - 1, 0)


def up_depth(cells):
    return pltpu.roll(cells, cells.shape[1] - 1, 1)


def up_second(cells, total_rows, depth_cells):
    first = pltpu.roll(cells[:total_rows], cells.shape[1] - depth_cells, 1)
    return jnp.concatenate([cells[total_rows:], first], axis=0)


def down_second(cells, total_rows, depth_cells):
    last = pltpu.roll(cells[-total_rows:], depth_cells, 1)
    return jnp.concatenate([last, cells[:-total_rows]], axis=0)


def swept(cells, along_x, along_y, along_z, total_rows, depth_cells):
    flux_x = along_x * (up_rows(cells) - cells)
    flux_y = along_y * (up_second(cells, total_rows, depth_cells) - cells)
    flux_z = along_z * (up_depth(cells) - cells)
    return (
        cells
        + (flux_x - pltpu.roll(flux_x, 1, 0))
        + (flux_y - down_second(flux_y, total_rows, depth_cells))
        + (flux_z - pltpu.roll(flux_z, 1, 1))
    )


def exchanged(cells, depth_cells):
    part, rows, lanes = cells.shape
    groups = lanes // depth_cells
    lane_group = lax.broadcasted_iota(jnp.int32, (rows, lanes), 1) // depth_cells
    out = []
    for first in range(0, part, groups):
        turned = cells[first : first + groups].reshape(groups * rows, lanes).T
        for a in range(groups):
            plane = None
            for b in range(groups):
                piece = turned[b * rows : (b + 1) * rows]
                moved = (b - a) % groups * depth_cells
                if moved:
                    piece = pltpu.roll(piece, moved, 1)
                plane = piece if plane is None else jnp.where(lane_group == b, piece, plane)
            out.append(plane)
    return jnp.stack(out)


def window(ref, slot, tiles, slab, margin):
    parts = []
    for step in (-1, 0, 1):
        at = lax.rem(slot + step + tiles, tiles) * slab
        parts.append(ref[:, pl.ds(pl.multiple_of(at, slab), slab), :])
    return jnp.concatenate(parts, axis=1)[:, slab - margin : 2 * slab + margin, :]


def second_kernel(
    depth_cells,
    blur_band,
    adjoint_band,
    recorded,
    *refs,
):
    *pieces, along_x, along_y, along_z, estimate, correction = refs
    pairs = len(pieces) // 2
    part, total_rows, lanes = recorded.shape
    flat = (part * total_rows, lanes)
    joined = [
        lax.rsqrt(lax.rsqrt(own[...] * exchanged(other[...], depth_cells)))
        for own, other in zip(pieces[:pairs], pieces[pairs:])
    ]
    joined = jnp.concatenate(joined, axis=0)
    cells = (recorded[...] * joined).reshape(flat)
    edges = [ref[...].reshape(flat) for ref in (along_x, along_y, along_z)]
    for _ in range(SWEEPS):
        cells = swept(cells, *edges, total_rows, depth_cells)
    estimate[...] = cells.reshape(estimate.shape)
    correction[...] = corrected(
        recorded[...].reshape(flat), cells, blur_band, adjoint_band
    ).reshape(correction.shape)


def windows_kernel(tiles, depth_cells, own, other, kept, sent, product):
    product[...] = own[...] * exchanged(other[...], depth_cells)
    slab = product.shape[1] // tiles
    slot = own_slot(tiles)
    kept[...] = window(product, slot, tiles, slab, SWEEPS)
    sent[...] = window(product, tiles - 1 - slot, tiles, slab, SWEEPS)


def near_kernel(tiles, estimate, along_x, along_y, along_z, *outs):
    slot = own_slot(tiles)
    slab = estimate.shape[1] // tiles
    for ref, out in zip((estimate, along_x, along_y, along_z), outs):
        out[...] = window(ref, slot, tiles, slab, SWEEPS)


def last_kernel(groups, depth_cells, estimate, kept, received, along_x, along_y, along_z, out, held):
    part, extent, lanes = estimate.shape
    slab = extent - 2 * SWEEPS
    flat = (part * extent, lanes)
    joined = lax.rsqrt(lax.rsqrt(kept[...] * received[...]))
    cells = (estimate[...] * joined).reshape(flat)
    edges = [ref[...].reshape(flat) for ref in (along_x, along_y, along_z)]
    for _ in range(SWEEPS):
        cells = swept(cells, *edges, extent, depth_cells)
    cells = cells.reshape(part, extent, lanes)[:, SWEEPS : SWEEPS + slab]
    cells = cells.reshape(part * slab, lanes)
    cells = jnp.take_along_axis(cells, lane_order(cells.shape, depth_cells), axis=1)
    cells = cells.reshape(part, slab, lanes)
    cells = jnp.concatenate(
        [cells[:, :, g * depth_cells : (g + 1) * depth_cells] for g in range(groups)], axis=0
    )
    held[...] = jnp.swapaxes(cells, 0, 1)
    turn = rows_reversed()
    for i in range(slab):
        out[0, i] = held[jnp.where(turn, slab - 1 - i, i)]


def whole_views(data, labels, kernel, offsets):
    tiles = lax.axis_size("tile")
    _, slab, rows, depth_cells = data.shape
    groups = LANES // depth_cells
    part = rows // groups
    total_rows = slab * tiles
    extent = slab + 2 * SWEEPS
    f32 = jnp.float32
    block = (part, slab, LANES)
    view = (part, total_rows, LANES)
    near = (part, extent, LANES)
    vmem = pl.BlockSpec(memory_space=pltpu.VMEM)

    def call(body, outs, scratch, *args):
        shapes = tuple(jax.ShapeDtypeStruct(s, d) for s, d in outs)
        return pl.pallas_call(
            body,
            out_shape=shapes,
            in_specs=[vmem] * len(args),
            out_specs=tuple(vmem for _ in shapes),
            scratch_shapes=scratch,
            compiler_params=pltpu.CompilerParams(vmem_limit_bytes=32 << 20),
        )(*args)

    def across(cells, k):
        return lax.ppermute(cells, "tile", [(i, i ^ k) for i in range(tiles)])

    def swap(cells, bit):
        return lax.ppermute(cells, "view", [(i, i ^ bit) for i in range(VIEWS)])

    packed, both = call(
        functools.partial(pack_kernel, groups),
        [(block, f32), ((2 * part,) + block[1:], f32)],
        [pltpu.VMEM(data.shape[1:], f32), pltpu.VMEM(data.shape[1:], jnp.int32)],
        data,
        labels,
    )
    bands = call(band_kernel, [((2 * LANES, 2 * LANES), jnp.bfloat16)] * 2, [], kernel, offsets)
    blocks = [packed] + [across(both if k == LABELS_WITH else packed, k) for k in range(1, tiles)]
    two = ((2 * part,) + block[1:], f32)
    (near_labels,) = call(relay_kernel, [two], [], both, blocks[LABELS_WITH])
    made = [
        call(blocks_kernel, [two], [], *bands, *blocks[:2])[0],
        call(blocks_kernel, [two], [], *bands, *blocks[2:])[0],
    ]
    opposite = [swap(cells, 2) for cells in made]
    pieces = part // groups
    products = call(
        functools.partial(pair_kernel, tiles),
        [((groups,) + view[1:], f32)] * pieces,
        [],
        *made,
        *opposite,
    )
    (recorded,) = call(
        functools.partial(recorded_kernel, tiles),
        [(view, f32)],
        [],
        *blocks,
    )
    far_labels = across(near_labels, LABELS_BY)
    others = [swap(product, 1) for product in products]
    edges = call(
        functools.partial(edges_kernel, tiles, depth_cells),
        [(view, f32)] * 3,
        [pltpu.VMEM(view, f32)],
        near_labels,
        far_labels,
    )
    estimate, correction = call(
        functools.partial(second_kernel, depth_cells),
        [(view, f32)] * 2,
        [],
        *bands,
        recorded,
        *products,
        *others,
        *edges,
    )
    other = swap(correction, 1)
    near_cells = call(
        functools.partial(near_kernel, tiles), [(near, f32)] * 4, [], estimate, *edges
    )
    kept, sent = call(
        functools.partial(windows_kernel, tiles, depth_cells),
        [(near, f32)] * 2,
        [pltpu.VMEM(view, f32)],
        correction,
        other,
    )
    received = swap(sent, 2)
    (out,) = call(
        functools.partial(last_kernel, groups, depth_cells),
        [(data.shape, f32)],
        [pltpu.VMEM(data.shape[1:], f32)],
        near_cells[0],
        kept,
        received,
        *near_cells[1:],
    )
    return out


def fits_whole(shape):
    _, slab, rows, depth_cells = shape
    tiles = lax.axis_size("tile")
    return (
        lax.axis_size("view") == VIEWS
        and ITERS == 2
        and slab % ROWS == 0
        and slab >= SWEEPS
        and slab * tiles == depth_cells
        and tiles == 4
        and LANES % depth_cells == 0
        and rows % (LANES // depth_cells) ** 2 == 0
        and (2 * SWEEPS) % ROWS == 0
    )


def on_device(data, labels, kernel, offsets):
    form = whole_views if fits_whole(data.shape) else by_slabs
    return form(data, labels, kernel, offsets)


def solution(mesh):
    placed = (
        P(("parts", "view"), "tile", None, None),
        P(("parts", "view"), "tile", None, None),
        P("view", None, None),
        P("view", None),
    )
    return jax.shard_map(
        on_device,
        mesh=mesh,
        in_specs=placed,
        out_specs=P(("parts", "view"), "tile", None, None),
        check_vma=False,
    )
```

```python
import functools

import jax
import jax.experimental.pallas as pl
import jax.experimental.pallas.tpu as pltpu
import jax.numpy as jnp
from jax import lax
from jax.sharding import PartitionSpec as P

ITERS = 2
SWEEPS = 4

WEAK = 0.2
TAU = 0.15

LANES = 128
ROWS = 8
VIEWS = 4
SHARES = 7

LABELS_WITH = 3
LABELS_BY = 1


def extended(cells, sides, width):
    for axis, dim in sides:
        count = lax.axis_size(axis)
        ends = count - 1
        head = lax.slice_in_dim(cells, 0, width, axis=dim)
        tail = lax.slice_in_dim(cells, cells.shape[dim] - width, cells.shape[dim], axis=dim)
        cells = jnp.concatenate(
            [
                lax.ppermute(tail, axis, [(i, (i + 1) % count) for i in range(ends)]),
                cells,
                lax.ppermute(head, axis, [((i + 1) % count, i) for i in range(ends)]),
            ],
            axis=dim,
        )
    return cells


def swapped(block, axis, stride):
    count = lax.axis_size(axis)
    route = []
    for low in range(count):
        high = low | 1 << stride
        if high != low and high < count:
            route += [(low, high), (high, low)]
    return lax.ppermute(block, axis, route)


def band(kernel, offsets):
    depth_cells = kernel.shape[0]
    taps = jnp.arange(kernel.shape[1], dtype=jnp.int32) - 4
    depth = jnp.arange(depth_cells, dtype=jnp.int32)
    index = jnp.clip(depth[:, None] + taps[None, :] + offsets[:, None], 0, depth_cells - 1)
    weight = kernel / jnp.sum(kernel, axis=1, keepdims=True)
    return (index, weight)


def axis_term(field, region, axis):
    count = field.shape[axis]
    upper = lax.slice_in_dim(field, 1, count, axis=axis)
    lower = lax.slice_in_dim(field, 0, count - 1, axis=axis)
    same = jnp.where(
        lax.slice_in_dim(region, 1, count, axis=axis)
        == lax.slice_in_dim(region, 0, count - 1, axis=axis),
        1.0,
        WEAK,
    )
    flux = same * (upper - lower)
    after = [(0, 0)] * 3
    before = [(0, 0)] * 3
    after[axis] = (0, 1)
    before[axis] = (1, 0)
    return jnp.pad(flux, after) - jnp.pad(flux, before)


def sweep_rows(field, region, first_row, total_rows):
    extent = field.shape[0]
    global_rows = first_row + jnp.arange(extent, dtype=jnp.int32)
    inside = ((global_rows >= 0) & (global_rows < total_rows)).astype(field.dtype)[:, None, None]
    same = jnp.where(region[1:] == region[:-1], 1.0, WEAK) * inside[1:] * inside[:-1]
    flux = same * (field[1:] - field[:-1])
    inner = field[1:-1]
    inner_labels = region[1:-1]
    total = (
        flux[1:] - flux[:-1] + axis_term(inner, inner_labels, 1) + axis_term(inner, inner_labels, 2)
    )
    return inner + TAU * total


def regroup(received, tiles):
    slab, rows, depth_cells = received.shape
    blocks = received.reshape(slab, rows, tiles, depth_cells // tiles)
    return blocks.transpose(3, 1, 2, 0).reshape(depth_cells // tiles, rows, depth_cells)


def by_slabs(data, labels, kernel, offsets):
    recorded = data[0]
    region = labels[0]
    index, weight = band(kernel[0], offsets[0])
    tiles = lax.axis_size("tile")
    slab, rows, depth_cells = recorded.shape
    total_rows = slab * tiles
    start = lax.axis_index("tile") * slab
    parity = lax.axis_index("view") % 2
    columns = jnp.arange(depth_cells, dtype=jnp.int32)
    matrix = jnp.sum(weight[:, :, None] * (index[:, :, None] == columns[None, None, :]), axis=1)
    label_ext = extended(region, (("tile", 0),), SWEEPS)
    views = lax.axis_size("view")
    half_turn = [
        (v * tiles + t, (v + 2) % views * tiles + tiles - 1 - t)
        for v in range(views)
        for t in range(tiles)
    ]
    current = recorded
    for step in range(ITERS):
        forward_flat = jnp.dot(
            current.reshape(-1, depth_cells), matrix.T, precision=lax.Precision.HIGHEST
        )
        field = recorded / forward_flat.reshape(current.shape)
        flat = jnp.dot(field.reshape(-1, depth_cells), matrix, precision=lax.Precision.HIGHEST)
        correction = flat.reshape(field.shape)
        turned = jnp.flip(lax.ppermute(correction, ("view", "tile"), half_turn), (0, 2))
        paired = jnp.sqrt(correction * turned)
        outgoing = jnp.where(parity == 0, jnp.flip(paired, 2), paired)
        rotated = regroup(
            lax.all_to_all(outgoing, "tile", split_axis=2, concat_axis=2, tiled=True), tiles
        )
        rotated = jnp.where(parity == 1, jnp.flip(rotated, 2), rotated)
        partner = swapped(rotated, "view", 0)
        current = current * jnp.sqrt(paired * partner)
        widened = extended(current, (("tile", 0),), SWEEPS)
        for sweep in range(SWEEPS):
            extent = widened.shape[0]
            widened = sweep_rows(
                widened,
                label_ext[sweep : sweep + extent],
                start - SWEEPS + sweep,
                total_rows,
            )
        current = widened
    return current[None]


def rows_reversed():
    v = lax.axis_index("view")
    return lax.rem(v + 1, VIEWS) >= 2


def depth_reversed():
    return lax.axis_index("view") >= 2


def own_slot(tiles):
    t = lax.axis_index("tile")
    return jnp.where(rows_reversed(), tiles - 1 - t, t)


def lane_order(shape, depth_cells):
    lane = lax.broadcasted_iota(jnp.int32, shape, 1)
    base = lane // depth_cells * depth_cells
    return jnp.where(depth_reversed(), base + (base + depth_cells - 1 - lane), lane)


def pack_one(source, held, target, groups):
    slab, rows, depth_cells = held.shape
    turn = rows_reversed()
    for i in range(slab):
        held[i] = source[0, jnp.where(turn, slab - 1 - i, i)]
    part = rows // groups
    cells = jnp.swapaxes(held[...], 0, 1)
    cells = jnp.concatenate([cells[g * part : (g + 1) * part] for g in range(groups)], axis=2)
    flat = cells.reshape(part * slab, groups * depth_cells)
    order = lane_order(flat.shape, depth_cells)
    flat = jnp.take_along_axis(flat, order, axis=1)
    target[...] = flat.reshape(target.shape).astype(target.dtype)


def pack_kernel(groups, data, labels, data_out, both_out, held, held_labels):
    pack_one(data, held, data_out, groups)
    part = data_out.shape[0]
    both_out[:part] = data_out[...]
    pack_one(labels, held_labels, both_out.at[part:], groups)


def split(cells):
    high = cells.astype(jnp.bfloat16)
    return high, (cells - high.astype(jnp.float32)).astype(jnp.bfloat16)


def band_kernel(kernel, offsets, blur_out, adjoint_out):
    depth_cells, taps = kernel.shape[1:]
    span = blur_out.shape[0] // 2
    turn = depth_reversed()
    row = lax.broadcasted_iota(jnp.int32, (depth_cells, depth_cells), 0)
    col = lax.broadcasted_iota(jnp.int32, (depth_cells, depth_cells), 1)
    pick = col == jnp.where(turn, depth_cells - 1 - row, row)
    shift = jnp.sum(
        jnp.where(pick, jnp.broadcast_to(offsets[...], pick.shape), 0), axis=1, keepdims=True
    )
    depth = row[:, :1]
    depth = jnp.where(turn, depth_cells - 1 - depth, depth)
    taps_by_row = jnp.dot(
        pick.astype(jnp.float32),
        kernel[0],
        precision=lax.Precision.HIGHEST,
        preferred_element_type=jnp.float32,
    )
    weight = taps_by_row / jnp.sum(taps_by_row, axis=1, keepdims=True)
    lane = lax.broadcasted_iota(jnp.int32, (depth_cells, span), 1)
    within = lax.rem(lane, depth_cells)
    within = jnp.where(turn, depth_cells - 1 - within, within)
    total = jnp.zeros((depth_cells, span), jnp.float32)
    for k in range(taps):
        index = jnp.clip(depth + (k - 4) + shift, 0, depth_cells - 1)
        total = total + jnp.where(index == within, weight[:, k : k + 1], 0.0)
    matrix = jnp.concatenate(
        [jnp.where(lane // depth_cells == g, total, 0.0) for g in range(span // depth_cells)], axis=0
    )
    for cells, out in ((matrix.T, blur_out), (matrix, adjoint_out)):
        high, low = split(cells)
        for half in range(2):
            out[half * span : (half + 1) * span, :span] = high
            out[half * span : (half + 1) * span, span:] = low


def banded(cells, band):
    high, low = split(cells)
    both = jnp.dot(
        jnp.concatenate([high, low], axis=1), band[...], preferred_element_type=jnp.float32
    )
    lanes = cells.shape[1]
    return both[:, :lanes] + both[:, lanes:]


def corrected(recorded, estimate, blur_band, adjoint_band):
    return banded(recorded / banded(estimate, blur_band), adjoint_band)


def first_correction(block, blur_band, adjoint_band):
    flat = block.reshape(-1, block.shape[-1])
    return corrected(flat, flat, blur_band, adjoint_band).reshape(block.shape)


def place(target, slot, block):
    slab = block.shape[1]
    target[:, pl.ds(pl.multiple_of(slot * slab, slab), slab), :] = block


def blocks_kernel(blur_band, adjoint_band, *refs):
    blocks, correction = refs[:-1], refs[-1]
    part = correction.shape[0] // len(blocks)
    cells = jnp.concatenate([block[:part] for block in blocks], axis=0)
    correction[...] = first_correction(cells, blur_band, adjoint_band)


def relay_kernel(own_both, both, labels_out):
    part = both.shape[0] // 2
    labels_out[:part] = own_both[part:]
    labels_out[part:] = both[part:]


def pair_kernel(tiles, *refs):
    own, far, products = refs[:2], refs[2:4], refs[4:]
    pair = own[0].shape[0]
    part = pair // 2
    slot = own_slot(tiles)
    for k in range(tiles):
        mine, theirs = k * part, (tiles - 1 - k) * part
        near = own[mine // pair][mine % pair : mine % pair + part]
        cells = near * far[theirs // pair][theirs % pair : theirs % pair + part]
        for i, product in enumerate(products):
            size = product.shape[0]
            place(product, slot ^ k, cells[i * size : (i + 1) * size])


def recorded_kernel(tiles, *refs):
    blocks, recorded = refs[:-1], refs[-1]
    slot = own_slot(tiles)
    for k, ref in enumerate(blocks):
        place(recorded, slot ^ k, ref[: recorded.shape[0]])


def weights_kernel(tiles, depth_cells, near, far, *refs):
    outs, whole = refs[:-1], refs[-1]
    slot = own_slot(tiles)
    slab, lanes = near.shape[1:]
    part = near.shape[0] // 2
    for k in range(tiles):
        if k in (0, LABELS_WITH):
            cells = near[part:] if k else near[:part]
        else:
            cells = far[:part] if k == LABELS_BY else far[part:]
        place(whole, slot ^ k, cells)
    total_rows = tiles * slab
    region = whole[...].reshape(part * total_rows, lanes)
    row = lax.broadcasted_iota(jnp.int32, region.shape, 0)
    lane = lax.broadcasted_iota(jnp.int32, region.shape, 1)

    def weighted(upper, inside):
        same = jnp.where(upper == region, TAU, TAU * WEAK)
        return jnp.where(inside, same, 0.0)

    along_x = weighted(up_rows(region), lax.rem(row, total_rows) != total_rows - 1)
    along_y = weighted(
        up_second(region, total_rows, depth_cells),
        (row < (part - 1) * total_rows) | (lane < lanes - depth_cells),
    )
    along_z = weighted(up_depth(region), lax.rem(lane, depth_cells) != depth_cells - 1)
    shares = [
        along_x,
        down_rows(along_x),
        along_y,
        down_second(along_y, total_rows, depth_cells),
        along_z,
        down_depth(along_z),
    ]
    shares.append(1.0 - sum(shares[1:], shares[0]))
    for share, out in zip(shares, outs):
        out[...] = share.reshape(out.shape)


def up_rows(cells):
    return pltpu.roll(cells, cells.shape[0] - 1, 0)


def up_depth(cells):
    return pltpu.roll(cells, cells.shape[1] - 1, 1)


def up_second(cells, total_rows, depth_cells):
    first = pltpu.roll(cells[:total_rows], cells.shape[1] - depth_cells, 1)
    return jnp.concatenate([cells[total_rows:], first], axis=0)


def down_second(cells, total_rows, depth_cells):
    last = pltpu.roll(cells[-total_rows:], depth_cells, 1)
    return jnp.concatenate([last, cells[:-total_rows]], axis=0)


def down_rows(cells):
    return pltpu.roll(cells, 1, 0)


def down_depth(cells):
    return pltpu.roll(cells, 1, 1)


def swept(cells, shares, total_rows, depth_cells):
    up_x, down_x, up_y, down_y, up_z, down_z, kept = [
        ref[...].reshape(cells.shape) for ref in shares
    ]
    return (
        (up_z * up_depth(cells) + down_z * down_depth(cells))
        + (up_x * up_rows(cells) + down_x * down_rows(cells))
        + (
            up_y * up_second(cells, total_rows, depth_cells)
            + down_y * down_second(cells, total_rows, depth_cells)
        )
        + kept * cells
    )


def exchanged(cells, depth_cells):
    part, rows, lanes = cells.shape
    groups = lanes // depth_cells
    lane_group = lax.broadcasted_iota(jnp.int32, (rows, lanes), 1) // depth_cells
    out = []
    for first in range(0, part, groups):
        turned = cells[first : first + groups].reshape(groups * rows, lanes).T
        for a in range(groups):
            plane = None
            for b in range(groups):
                piece = turned[b * rows : (b + 1) * rows]
                moved = (b - a) % groups * depth_cells
                if moved:
                    piece = pltpu.roll(piece, moved, 1)
                plane = piece if plane is None else jnp.where(lane_group == b, piece, plane)
            out.append(plane)
    return jnp.stack(out)


def window(ref, slot, tiles, slab, margin):
    parts = []
    for step in (-1, 0, 1):
        at = lax.rem(slot + step + tiles, tiles) * slab
        parts.append(ref[:, pl.ds(pl.multiple_of(at, slab), slab), :])
    return jnp.concatenate(parts, axis=1)[:, slab - margin : 2 * slab + margin, :]


def second_kernel(
    depth_cells,
    blur_band,
    adjoint_band,
    recorded,
    *refs,
):
    refs, (estimate, correction) = refs[:-2], refs[-2:]
    pieces, shares = refs[:-SHARES], refs[-SHARES:]
    pairs = len(pieces) // 2
    part, total_rows, lanes = recorded.shape
    flat = (part * total_rows, lanes)
    joined = [
        lax.rsqrt(lax.rsqrt(own[...] * exchanged(other[...], depth_cells)))
        for own, other in zip(pieces[:pairs], pieces[pairs:])
    ]
    joined = jnp.concatenate(joined, axis=0)
    cells = (recorded[...] * joined).reshape(flat)
    for _ in range(SWEEPS):
        cells = swept(cells, shares, total_rows, depth_cells)
    estimate[...] = cells.reshape(estimate.shape)
    correction[...] = corrected(
        recorded[...].reshape(flat), cells, blur_band, adjoint_band
    ).reshape(correction.shape)


def windows_kernel(tiles, depth_cells, own, other, kept, sent, product):
    product[...] = own[...] * exchanged(other[...], depth_cells)
    slab = product.shape[1] // tiles
    slot = own_slot(tiles)
    kept[...] = window(product, slot, tiles, slab, SWEEPS)
    sent[...] = window(product, tiles - 1 - slot, tiles, slab, SWEEPS)


def near_kernel(tiles, *refs):
    slot = own_slot(tiles)
    slab = refs[0].shape[1] // tiles
    half = len(refs) // 2
    for ref, out in zip(refs[:half], refs[half:]):
        out[...] = window(ref, slot, tiles, slab, SWEEPS)


def last_kernel(groups, depth_cells, estimate, kept, received, *refs):
    *shares, out, held = refs
    part, extent, lanes = estimate.shape
    slab = extent - 2 * SWEEPS
    flat = (part * extent, lanes)
    joined = lax.rsqrt(lax.rsqrt(kept[...] * received[...]))
    cells = (estimate[...] * joined).reshape(flat)
    for _ in range(SWEEPS):
        cells = swept(cells, shares, extent, depth_cells)
    cells = cells.reshape(part, extent, lanes)[:, SWEEPS : SWEEPS + slab]
    cells = cells.reshape(part * slab, lanes)
    cells = jnp.take_along_axis(cells, lane_order(cells.shape, depth_cells), axis=1)
    cells = cells.reshape(part, slab, lanes)
    cells = jnp.concatenate(
        [cells[:, :, g * depth_cells : (g + 1) * depth_cells] for g in range(groups)], axis=0
    )
    held[...] = jnp.swapaxes(cells, 0, 1)
    turn = rows_reversed()
    for i in range(slab):
        out[0, i] = held[jnp.where(turn, slab - 1 - i, i)]


def whole_views(data, labels, kernel, offsets):
    tiles = lax.axis_size("tile")
    _, slab, rows, depth_cells = data.shape
    groups = LANES // depth_cells
    part = rows // groups
    total_rows = slab * tiles
    extent = slab + 2 * SWEEPS
    f32 = jnp.float32
    block = (part, slab, LANES)
    view = (part, total_rows, LANES)
    near = (part, extent, LANES)
    vmem = pl.BlockSpec(memory_space=pltpu.VMEM)

    def call(body, outs, scratch, *args):
        shapes = tuple(jax.ShapeDtypeStruct(s, d) for s, d in outs)
        return pl.pallas_call(
            body,
            out_shape=shapes,
            in_specs=[vmem] * len(args),
            out_specs=tuple(vmem for _ in shapes),
            scratch_shapes=scratch,
            compiler_params=pltpu.CompilerParams(vmem_limit_bytes=32 << 20),
        )(*args)

    def across(cells, k):
        return lax.ppermute(cells, "tile", [(i, i ^ k) for i in range(tiles)])

    def swap(cells, bit):
        return lax.ppermute(cells, "view", [(i, i ^ bit) for i in range(VIEWS)])

    packed, both = call(
        functools.partial(pack_kernel, groups),
        [(block, f32), ((2 * part,) + block[1:], f32)],
        [pltpu.VMEM(data.shape[1:], f32), pltpu.VMEM(data.shape[1:], jnp.int32)],
        data,
        labels,
    )
    bands = call(band_kernel, [((2 * LANES, 2 * LANES), jnp.bfloat16)] * 2, [], kernel, offsets)
    blocks = [packed] + [across(both if k == LABELS_WITH else packed, k) for k in range(1, tiles)]
    two = ((2 * part,) + block[1:], f32)
    (near_labels,) = call(relay_kernel, [two], [], both, blocks[LABELS_WITH])
    made = [
        call(blocks_kernel, [two], [], *bands, *blocks[:2])[0],
        call(blocks_kernel, [two], [], *bands, *blocks[2:])[0],
    ]
    opposite = [swap(cells, 2) for cells in made]
    pieces = part // groups
    products = call(
        functools.partial(pair_kernel, tiles),
        [((groups,) + view[1:], f32)] * pieces,
        [],
        *made,
        *opposite,
    )
    (recorded,) = call(
        functools.partial(recorded_kernel, tiles),
        [(view, f32)],
        [],
        *blocks,
    )
    far_labels = across(near_labels, LABELS_BY)
    others = [swap(product, 1) for product in products]
    shares = call(
        functools.partial(weights_kernel, tiles, depth_cells),
        [(view, f32)] * SHARES,
        [pltpu.VMEM(view, f32)],
        near_labels,
        far_labels,
    )
    estimate, correction = call(
        functools.partial(second_kernel, depth_cells),
        [(view, f32)] * 2,
        [],
        *bands,
        recorded,
        *products,
        *others,
        *shares,
    )
    other = swap(correction, 1)
    near_cells = call(
        functools.partial(near_kernel, tiles), [(near, f32)] * (1 + SHARES), [], estimate, *shares
    )
    kept, sent = call(
        functools.partial(windows_kernel, tiles, depth_cells),
        [(near, f32)] * 2,
        [pltpu.VMEM(view, f32)],
        correction,
        other,
    )
    received = swap(sent, 2)
    (out,) = call(
        functools.partial(last_kernel, groups, depth_cells),
        [(data.shape, f32)],
        [pltpu.VMEM(data.shape[1:], f32)],
        near_cells[0],
        kept,
        received,
        *near_cells[1:],
    )
    return out


def fits_whole(shape):
    _, slab, rows, depth_cells = shape
    tiles = lax.axis_size("tile")
    return (
        lax.axis_size("view") == VIEWS
        and ITERS == 2
        and slab % ROWS == 0
        and slab >= SWEEPS
        and slab * tiles == depth_cells
        and tiles == 4
        and LANES % depth_cells == 0
        and rows % (LANES // depth_cells) ** 2 == 0
        and (2 * SWEEPS) % ROWS == 0
    )


def on_device(data, labels, kernel, offsets):
    form = whole_views if fits_whole(data.shape) else by_slabs
    return form(data, labels, kernel, offsets)


def solution(mesh):
    placed = (
        P(("parts", "view"), "tile", None, None),
        P(("parts", "view"), "tile", None, None),
        P("view", None, None),
        P("view", None),
    )
    return jax.shard_map(
        on_device,
        mesh=mesh,
        in_specs=placed,
        out_specs=P(("parts", "view"), "tile", None, None),
        check_vma=False,
    )
```

```python
import functools

import jax
import jax.experimental.pallas as pl
import jax.experimental.pallas.tpu as pltpu
import jax.numpy as jnp
from jax import lax
from jax.sharding import PartitionSpec as P

ITERS = 2
SWEEPS = 4

WEAK = 0.2
TAU = 0.15

LANES = 128
ROWS = 8
VIEWS = 4
SHARES = 7

LABELS_WITH = 3
LABELS_BY = 1


def extended(cells, sides, width):
    for axis, dim in sides:
        count = lax.axis_size(axis)
        ends = count - 1
        head = lax.slice_in_dim(cells, 0, width, axis=dim)
        tail = lax.slice_in_dim(cells, cells.shape[dim] - width, cells.shape[dim], axis=dim)
        cells = jnp.concatenate(
            [
                lax.ppermute(tail, axis, [(i, (i + 1) % count) for i in range(ends)]),
                cells,
                lax.ppermute(head, axis, [((i + 1) % count, i) for i in range(ends)]),
            ],
            axis=dim,
        )
    return cells


def swapped(block, axis, stride):
    count = lax.axis_size(axis)
    route = []
    for low in range(count):
        high = low | 1 << stride
        if high != low and high < count:
            route += [(low, high), (high, low)]
    return lax.ppermute(block, axis, route)


def band(kernel, offsets):
    depth_cells = kernel.shape[0]
    taps = jnp.arange(kernel.shape[1], dtype=jnp.int32) - 4
    depth = jnp.arange(depth_cells, dtype=jnp.int32)
    index = jnp.clip(depth[:, None] + taps[None, :] + offsets[:, None], 0, depth_cells - 1)
    weight = kernel / jnp.sum(kernel, axis=1, keepdims=True)
    return (index, weight)


def axis_term(field, region, axis):
    count = field.shape[axis]
    upper = lax.slice_in_dim(field, 1, count, axis=axis)
    lower = lax.slice_in_dim(field, 0, count - 1, axis=axis)
    same = jnp.where(
        lax.slice_in_dim(region, 1, count, axis=axis)
        == lax.slice_in_dim(region, 0, count - 1, axis=axis),
        1.0,
        WEAK,
    )
    flux = same * (upper - lower)
    after = [(0, 0)] * 3
    before = [(0, 0)] * 3
    after[axis] = (0, 1)
    before[axis] = (1, 0)
    return jnp.pad(flux, after) - jnp.pad(flux, before)


def sweep_rows(field, region, first_row, total_rows):
    extent = field.shape[0]
    global_rows = first_row + jnp.arange(extent, dtype=jnp.int32)
    inside = ((global_rows >= 0) & (global_rows < total_rows)).astype(field.dtype)[:, None, None]
    same = jnp.where(region[1:] == region[:-1], 1.0, WEAK) * inside[1:] * inside[:-1]
    flux = same * (field[1:] - field[:-1])
    inner = field[1:-1]
    inner_labels = region[1:-1]
    total = (
        flux[1:] - flux[:-1] + axis_term(inner, inner_labels, 1) + axis_term(inner, inner_labels, 2)
    )
    return inner + TAU * total


def regroup(received, tiles):
    slab, rows, depth_cells = received.shape
    blocks = received.reshape(slab, rows, tiles, depth_cells // tiles)
    return blocks.transpose(3, 1, 2, 0).reshape(depth_cells // tiles, rows, depth_cells)


def by_slabs(data, labels, kernel, offsets):
    recorded = data[0]
    region = labels[0]
    index, weight = band(kernel[0], offsets[0])
    tiles = lax.axis_size("tile")
    slab, rows, depth_cells = recorded.shape
    total_rows = slab * tiles
    start = lax.axis_index("tile") * slab
    parity = lax.axis_index("view") % 2
    columns = jnp.arange(depth_cells, dtype=jnp.int32)
    matrix = jnp.sum(weight[:, :, None] * (index[:, :, None] == columns[None, None, :]), axis=1)
    label_ext = extended(region, (("tile", 0),), SWEEPS)
    views = lax.axis_size("view")
    half_turn = [
        (v * tiles + t, (v + 2) % views * tiles + tiles - 1 - t)
        for v in range(views)
        for t in range(tiles)
    ]
    current = recorded
    for step in range(ITERS):
        forward_flat = jnp.dot(
            current.reshape(-1, depth_cells), matrix.T, precision=lax.Precision.HIGHEST
        )
        field = recorded / forward_flat.reshape(current.shape)
        flat = jnp.dot(field.reshape(-1, depth_cells), matrix, precision=lax.Precision.HIGHEST)
        correction = flat.reshape(field.shape)
        turned = jnp.flip(lax.ppermute(correction, ("view", "tile"), half_turn), (0, 2))
        paired = jnp.sqrt(correction * turned)
        outgoing = jnp.where(parity == 0, jnp.flip(paired, 2), paired)
        rotated = regroup(
            lax.all_to_all(outgoing, "tile", split_axis=2, concat_axis=2, tiled=True), tiles
        )
        rotated = jnp.where(parity == 1, jnp.flip(rotated, 2), rotated)
        partner = swapped(rotated, "view", 0)
        current = current * jnp.sqrt(paired * partner)
        widened = extended(current, (("tile", 0),), SWEEPS)
        for sweep in range(SWEEPS):
            extent = widened.shape[0]
            widened = sweep_rows(
                widened,
                label_ext[sweep : sweep + extent],
                start - SWEEPS + sweep,
                total_rows,
            )
        current = widened
    return current[None]


def rows_reversed():
    v = lax.axis_index("view")
    return lax.rem(v + 1, VIEWS) >= 2


def depth_reversed():
    return lax.axis_index("view") >= 2


def own_slot(tiles):
    t = lax.axis_index("tile")
    return jnp.where(rows_reversed(), tiles - 1 - t, t)


def lane_order(shape, depth_cells):
    lane = lax.broadcasted_iota(jnp.int32, shape, 1)
    base = lane // depth_cells * depth_cells
    return jnp.where(depth_reversed(), base + (base + depth_cells - 1 - lane), lane)


def pack_one(source, held, target, groups):
    slab, rows, depth_cells = held.shape
    turn = rows_reversed()
    for i in range(slab):
        held[i] = source[0, jnp.where(turn, slab - 1 - i, i)]
    part = rows // groups
    cells = jnp.swapaxes(held[...], 0, 1)
    cells = jnp.concatenate([cells[g * part : (g + 1) * part] for g in range(groups)], axis=2)
    flat = cells.reshape(part * slab, groups * depth_cells)
    order = lane_order(flat.shape, depth_cells)
    flat = jnp.take_along_axis(flat, order, axis=1)
    target[...] = flat.reshape(target.shape).astype(target.dtype)


def pack_kernel(groups, data, labels, data_out, both_out, held, held_labels):
    pack_one(data, held, data_out, groups)
    part = data_out.shape[0]
    both_out[:part] = data_out[...]
    pack_one(labels, held_labels, both_out.at[part:], groups)


def split(cells):
    high = cells.astype(jnp.bfloat16)
    return high, (cells - high.astype(jnp.float32)).astype(jnp.bfloat16)


def band_kernel(kernel, offsets, blur_out, adjoint_out):
    depth_cells, taps = kernel.shape[1:]
    span = blur_out.shape[0] // 2
    turn = depth_reversed()
    row = lax.broadcasted_iota(jnp.int32, (depth_cells, depth_cells), 0)
    col = lax.broadcasted_iota(jnp.int32, (depth_cells, depth_cells), 1)
    pick = col == jnp.where(turn, depth_cells - 1 - row, row)
    shift = jnp.sum(
        jnp.where(pick, jnp.broadcast_to(offsets[...], pick.shape), 0), axis=1, keepdims=True
    )
    depth = row[:, :1]
    depth = jnp.where(turn, depth_cells - 1 - depth, depth)
    taps_by_row = jnp.dot(
        pick.astype(jnp.float32),
        kernel[0],
        precision=lax.Precision.HIGHEST,
        preferred_element_type=jnp.float32,
    )
    weight = taps_by_row / jnp.sum(taps_by_row, axis=1, keepdims=True)
    lane = lax.broadcasted_iota(jnp.int32, (depth_cells, span), 1)
    within = lax.rem(lane, depth_cells)
    within = jnp.where(turn, depth_cells - 1 - within, within)
    total = jnp.zeros((depth_cells, span), jnp.float32)
    for k in range(taps):
        index = jnp.clip(depth + (k - 4) + shift, 0, depth_cells - 1)
        total = total + jnp.where(index == within, weight[:, k : k + 1], 0.0)
    matrix = jnp.concatenate(
        [jnp.where(lane // depth_cells == g, total, 0.0) for g in range(span // depth_cells)], axis=0
    )
    for cells, out in ((matrix.T, blur_out), (matrix, adjoint_out)):
        high, low = split(cells)
        for half in range(2):
            out[half * span : (half + 1) * span, :span] = high
            out[half * span : (half + 1) * span, span:] = low


def banded(cells, band):
    high, low = split(cells)
    both = jnp.dot(
        jnp.concatenate([high, low], axis=1), band[...], preferred_element_type=jnp.float32
    )
    lanes = cells.shape[1]
    return both[:, :lanes] + both[:, lanes:]


def corrected(recorded, estimate, blur_band, adjoint_band):
    return banded(recorded / banded(estimate, blur_band), adjoint_band)


def first_correction(block, blur_band, adjoint_band):
    flat = block.reshape(-1, block.shape[-1])
    return corrected(flat, flat, blur_band, adjoint_band).reshape(block.shape)


def place(target, slot, block):
    slab = block.shape[1]
    target[:, pl.ds(pl.multiple_of(slot * slab, slab), slab), :] = block


def blocks_kernel(blur_band, adjoint_band, *refs):
    blocks, correction = refs[:-1], refs[-1]
    part = correction.shape[0] // len(blocks)
    cells = jnp.concatenate([block[:part] for block in blocks], axis=0)
    correction[...] = first_correction(cells, blur_band, adjoint_band)


def relay_kernel(own_both, both, labels_out):
    part = both.shape[0] // 2
    labels_out[:part] = own_both[part:]
    labels_out[part:] = both[part:]


def pair_kernel(tiles, *refs):
    own, far, products = refs[:2], refs[2:4], refs[4:]
    pair = own[0].shape[0]
    part = pair // 2
    slot = own_slot(tiles)
    for k in range(tiles):
        mine, theirs = k * part, (tiles - 1 - k) * part
        near = own[mine // pair][mine % pair : mine % pair + part]
        cells = near * far[theirs // pair][theirs % pair : theirs % pair + part]
        for i, product in enumerate(products):
            size = product.shape[0]
            place(product, slot ^ k, cells[i * size : (i + 1) * size])


def recorded_kernel(tiles, *refs):
    blocks, recorded = refs[:-1], refs[-1]
    slot = own_slot(tiles)
    for k, ref in enumerate(blocks):
        place(recorded, slot ^ k, ref[: recorded.shape[0]])


def weights_kernel(tiles, depth_cells, near, far, *refs):
    outs, whole = refs[:-1], refs[-1]
    slot = own_slot(tiles)
    slab, lanes = near.shape[1:]
    part = near.shape[0] // 2
    for k in range(tiles):
        if k in (0, LABELS_WITH):
            cells = near[part:] if k else near[:part]
        else:
            cells = far[:part] if k == LABELS_BY else far[part:]
        place(whole, slot ^ k, cells)
    total_rows = tiles * slab
    region = whole[...].reshape(part * total_rows, lanes)
    row = lax.broadcasted_iota(jnp.int32, region.shape, 0)
    lane = lax.broadcasted_iota(jnp.int32, region.shape, 1)

    def weighted(upper, inside):
        same = jnp.where(upper == region, TAU, TAU * WEAK)
        return jnp.where(inside, same, 0.0)

    along_x = weighted(up_rows(region), lax.rem(row, total_rows) != total_rows - 1)
    along_y = weighted(
        up_second(region, total_rows, depth_cells),
        (row < (part - 1) * total_rows) | (lane < lanes - depth_cells),
    )
    along_z = weighted(up_depth(region), lax.rem(lane, depth_cells) != depth_cells - 1)
    shares = [
        along_x,
        down_rows(along_x),
        along_y,
        down_second(along_y, total_rows, depth_cells),
        along_z,
        down_depth(along_z),
    ]
    shares.append(1.0 - sum(shares[1:], shares[0]))
    for share, out in zip(shares, outs):
        out[...] = share.reshape(out.shape)


def up_rows(cells):
    return pltpu.roll(cells, cells.shape[0] - 1, 0)


def up_depth(cells):
    return pltpu.roll(cells, cells.shape[1] - 1, 1)


def up_second(cells, total_rows, depth_cells):
    first = pltpu.roll(cells[:total_rows], cells.shape[1] - depth_cells, 1)
    return jnp.concatenate([cells[total_rows:], first], axis=0)


def down_second(cells, total_rows, depth_cells):
    last = pltpu.roll(cells[-total_rows:], depth_cells, 1)
    return jnp.concatenate([last, cells[:-total_rows]], axis=0)


def down_rows(cells):
    return pltpu.roll(cells, 1, 0)


def down_depth(cells):
    return pltpu.roll(cells, 1, 1)


def swept(cells, shares, held, total_rows, depth_cells):
    up_x, down_x, up_y, down_y, up_z, down_z, kept = [
        ref[...].reshape(cells.shape) for ref in shares
    ]
    rows = cells.shape[0]
    held[ROWS : ROWS + rows] = cells
    return (
        (up_z * up_depth(cells) + down_z * down_depth(cells))
        + (up_x * held[ROWS + 1 : ROWS + 1 + rows] + down_x * held[ROWS - 1 : ROWS - 1 + rows])
        + (
            up_y * up_second(cells, total_rows, depth_cells)
            + down_y * down_second(cells, total_rows, depth_cells)
        )
        + kept * cells
    )


def exchanged(cells, depth_cells):
    part, rows, lanes = cells.shape
    groups = lanes // depth_cells
    lane_group = lax.broadcasted_iota(jnp.int32, (rows, lanes), 1) // depth_cells
    out = []
    for first in range(0, part, groups):
        turned = cells[first : first + groups].reshape(groups * rows, lanes).T
        for a in range(groups):
            plane = None
            for b in range(groups):
                piece = turned[b * rows : (b + 1) * rows]
                moved = (b - a) % groups * depth_cells
                if moved:
                    piece = pltpu.roll(piece, moved, 1)
                plane = piece if plane is None else jnp.where(lane_group == b, piece, plane)
            out.append(plane)
    return jnp.stack(out)


def window(ref, slot, tiles, slab, margin):
    parts = []
    for step in (-1, 0, 1):
        at = lax.rem(slot + step + tiles, tiles) * slab
        parts.append(ref[:, pl.ds(pl.multiple_of(at, slab), slab), :])
    return jnp.concatenate(parts, axis=1)[:, slab - margin : 2 * slab + margin, :]


def second_kernel(
    depth_cells,
    blur_band,
    adjoint_band,
    recorded,
    *refs,
):
    refs, (estimate, correction, shifted) = refs[:-3], refs[-3:]
    shifted[:ROWS] = jnp.zeros_like(shifted[:ROWS])
    shifted[-ROWS:] = jnp.zeros_like(shifted[-ROWS:])
    pieces, shares = refs[:-SHARES], refs[-SHARES:]
    pairs = len(pieces) // 2
    part, total_rows, lanes = recorded.shape
    flat = (part * total_rows, lanes)
    own, other = [
        jnp.concatenate([piece[...] for piece in half], axis=0)
        for half in (pieces[:pairs], pieces[pairs:])
    ]
    joined = lax.rsqrt(lax.rsqrt(own * exchanged(other, depth_cells)))
    cells = (recorded[...] * joined).reshape(flat)
    for _ in range(SWEEPS):
        cells = swept(cells, shares, shifted, total_rows, depth_cells)
    estimate[...] = cells.reshape(estimate.shape)
    correction[...] = corrected(
        recorded[...].reshape(flat), cells, blur_band, adjoint_band
    ).reshape(correction.shape)


def windows_kernel(tiles, depth_cells, own, other, kept, sent, product):
    product[...] = own[...] * exchanged(other[...], depth_cells)
    slab = product.shape[1] // tiles
    slot = own_slot(tiles)
    kept[...] = window(product, slot, tiles, slab, SWEEPS)
    sent[...] = window(product, tiles - 1 - slot, tiles, slab, SWEEPS)


def near_kernel(tiles, *refs):
    slot = own_slot(tiles)
    slab = refs[0].shape[1] // tiles
    half = len(refs) // 2
    for ref, out in zip(refs[:half], refs[half:]):
        out[...] = window(ref, slot, tiles, slab, SWEEPS)


def last_kernel(groups, depth_cells, estimate, kept, received, *refs):
    *shares, out, held, shifted = refs
    shifted[:ROWS] = jnp.zeros_like(shifted[:ROWS])
    shifted[-ROWS:] = jnp.zeros_like(shifted[-ROWS:])
    part, extent, lanes = estimate.shape
    slab = extent - 2 * SWEEPS
    flat = (part * extent, lanes)
    joined = lax.rsqrt(lax.rsqrt(kept[...] * received[...]))
    cells = (estimate[...] * joined).reshape(flat)
    for _ in range(SWEEPS):
        cells = swept(cells, shares, shifted, extent, depth_cells)
    cells = cells.reshape(part, extent, lanes)[:, SWEEPS : SWEEPS + slab]
    cells = cells.reshape(part * slab, lanes)
    cells = jnp.take_along_axis(cells, lane_order(cells.shape, depth_cells), axis=1)
    cells = cells.reshape(part, slab, lanes)
    cells = jnp.concatenate(
        [cells[:, :, g * depth_cells : (g + 1) * depth_cells] for g in range(groups)], axis=0
    )
    held[...] = jnp.swapaxes(cells, 0, 1)
    turn = rows_reversed()
    for i in range(slab):
        out[0, i] = held[jnp.where(turn, slab - 1 - i, i)]


def whole_views(data, labels, kernel, offsets):
    tiles = lax.axis_size("tile")
    _, slab, rows, depth_cells = data.shape
    groups = LANES // depth_cells
    part = rows // groups
    total_rows = slab * tiles
    extent = slab + 2 * SWEEPS
    f32 = jnp.float32
    block = (part, slab, LANES)
    view = (part, total_rows, LANES)
    near = (part, extent, LANES)
    vmem = pl.BlockSpec(memory_space=pltpu.VMEM)

    def call(body, outs, scratch, *args):
        shapes = tuple(jax.ShapeDtypeStruct(s, d) for s, d in outs)
        return pl.pallas_call(
            body,
            out_shape=shapes,
            in_specs=[vmem] * len(args),
            out_specs=tuple(vmem for _ in shapes),
            scratch_shapes=scratch,
            compiler_params=pltpu.CompilerParams(vmem_limit_bytes=32 << 20),
        )(*args)

    def across(cells, k):
        return lax.ppermute(cells, "tile", [(i, i ^ k) for i in range(tiles)])

    def swap(cells, bit):
        return lax.ppermute(cells, "view", [(i, i ^ bit) for i in range(VIEWS)])

    packed, both = call(
        functools.partial(pack_kernel, groups),
        [(block, f32), ((2 * part,) + block[1:], f32)],
        [pltpu.VMEM(data.shape[1:], f32), pltpu.VMEM(data.shape[1:], jnp.int32)],
        data,
        labels,
    )
    bands = call(band_kernel, [((2 * LANES, 2 * LANES), jnp.bfloat16)] * 2, [], kernel, offsets)
    blocks = [packed] + [across(both if k == LABELS_WITH else packed, k) for k in range(1, tiles)]
    two = ((2 * part,) + block[1:], f32)
    (near_labels,) = call(relay_kernel, [two], [], both, blocks[LABELS_WITH])
    made = [
        call(blocks_kernel, [two], [], *bands, *blocks[:2])[0],
        call(blocks_kernel, [two], [], *bands, *blocks[2:])[0],
    ]
    opposite = [swap(cells, 2) for cells in made]
    pieces = 2
    products = call(
        functools.partial(pair_kernel, tiles),
        [((part // pieces,) + view[1:], f32)] * pieces,
        [],
        *made,
        *opposite,
    )
    (recorded,) = call(
        functools.partial(recorded_kernel, tiles),
        [(view, f32)],
        [],
        *blocks,
    )
    far_labels = across(near_labels, LABELS_BY)
    others = [swap(product, 1) for product in products]
    shares = call(
        functools.partial(weights_kernel, tiles, depth_cells),
        [(view, f32)] * SHARES,
        [pltpu.VMEM(view, f32)],
        near_labels,
        far_labels,
    )
    estimate, correction = call(
        functools.partial(second_kernel, depth_cells),
        [(view, f32)] * 2,
        [pltpu.VMEM((part * total_rows + 2 * ROWS, LANES), f32)],
        *bands,
        recorded,
        *products,
        *others,
        *shares,
    )
    other = swap(correction, 1)
    near_cells = call(
        functools.partial(near_kernel, tiles), [(near, f32)] * (1 + SHARES), [], estimate, *shares
    )
    kept, sent = call(
        functools.partial(windows_kernel, tiles, depth_cells),
        [(near, f32)] * 2,
        [pltpu.VMEM(view, f32)],
        correction,
        other,
    )
    received = swap(sent, 2)
    (out,) = call(
        functools.partial(last_kernel, groups, depth_cells),
        [(data.shape, f32)],
        [pltpu.VMEM(data.shape[1:], f32), pltpu.VMEM((part * extent + 2 * ROWS, LANES), f32)],
        near_cells[0],
        kept,
        received,
        *near_cells[1:],
    )
    return out


def fits_whole(shape):
    _, slab, rows, depth_cells = shape
    tiles = lax.axis_size("tile")
    return (
        lax.axis_size("view") == VIEWS
        and ITERS == 2
        and slab % ROWS == 0
        and slab >= SWEEPS
        and slab * tiles == depth_cells
        and tiles == 4
        and LANES % depth_cells == 0
        and rows % (LANES // depth_cells) ** 2 == 0
        and (2 * SWEEPS) % ROWS == 0
    )


def on_device(data, labels, kernel, offsets):
    form = whole_views if fits_whole(data.shape) else by_slabs
    return form(data, labels, kernel, offsets)


def solution(mesh):
    placed = (
        P(("parts", "view"), "tile", None, None),
        P(("parts", "view"), "tile", None, None),
        P("view", None, None),
        P("view", None),
    )
    return jax.shard_map(
        on_device,
        mesh=mesh,
        in_specs=placed,
        out_specs=P(("parts", "view"), "tile", None, None),
        check_vma=False,
    )
```

```python
import functools

import jax
import jax.experimental.pallas as pl
import jax.experimental.pallas.tpu as pltpu
import jax.numpy as jnp
from jax import lax
from jax.sharding import PartitionSpec as P

ITERS = 2
SWEEPS = 4

WEAK = 0.2
TAU = 0.15

LANES = 128
ROWS = 8
VIEWS = 4
SHARES = 7

LABELS_WITH = 3
LABELS_BY = 1


def extended(cells, sides, width):
    for axis, dim in sides:
        count = lax.axis_size(axis)
        ends = count - 1
        head = lax.slice_in_dim(cells, 0, width, axis=dim)
        tail = lax.slice_in_dim(cells, cells.shape[dim] - width, cells.shape[dim], axis=dim)
        cells = jnp.concatenate(
            [
                lax.ppermute(tail, axis, [(i, (i + 1) % count) for i in range(ends)]),
                cells,
                lax.ppermute(head, axis, [((i + 1) % count, i) for i in range(ends)]),
            ],
            axis=dim,
        )
    return cells


def swapped(block, axis, stride):
    count = lax.axis_size(axis)
    route = []
    for low in range(count):
        high = low | 1 << stride
        if high != low and high < count:
            route += [(low, high), (high, low)]
    return lax.ppermute(block, axis, route)


def band(kernel, offsets):
    depth_cells = kernel.shape[0]
    taps = jnp.arange(kernel.shape[1], dtype=jnp.int32) - 4
    depth = jnp.arange(depth_cells, dtype=jnp.int32)
    index = jnp.clip(depth[:, None] + taps[None, :] + offsets[:, None], 0, depth_cells - 1)
    weight = kernel / jnp.sum(kernel, axis=1, keepdims=True)
    return (index, weight)


def axis_term(field, region, axis):
    count = field.shape[axis]
    upper = lax.slice_in_dim(field, 1, count, axis=axis)
    lower = lax.slice_in_dim(field, 0, count - 1, axis=axis)
    same = jnp.where(
        lax.slice_in_dim(region, 1, count, axis=axis)
        == lax.slice_in_dim(region, 0, count - 1, axis=axis),
        1.0,
        WEAK,
    )
    flux = same * (upper - lower)
    after = [(0, 0)] * 3
    before = [(0, 0)] * 3
    after[axis] = (0, 1)
    before[axis] = (1, 0)
    return jnp.pad(flux, after) - jnp.pad(flux, before)


def sweep_rows(field, region, first_row, total_rows):
    extent = field.shape[0]
    global_rows = first_row + jnp.arange(extent, dtype=jnp.int32)
    inside = ((global_rows >= 0) & (global_rows < total_rows)).astype(field.dtype)[:, None, None]
    same = jnp.where(region[1:] == region[:-1], 1.0, WEAK) * inside[1:] * inside[:-1]
    flux = same * (field[1:] - field[:-1])
    inner = field[1:-1]
    inner_labels = region[1:-1]
    total = (
        flux[1:] - flux[:-1] + axis_term(inner, inner_labels, 1) + axis_term(inner, inner_labels, 2)
    )
    return inner + TAU * total


def regroup(received, tiles):
    slab, rows, depth_cells = received.shape
    blocks = received.reshape(slab, rows, tiles, depth_cells // tiles)
    return blocks.transpose(3, 1, 2, 0).reshape(depth_cells // tiles, rows, depth_cells)


def by_slabs(data, labels, kernel, offsets):
    recorded = data[0]
    region = labels[0]
    index, weight = band(kernel[0], offsets[0])
    tiles = lax.axis_size("tile")
    slab, rows, depth_cells = recorded.shape
    total_rows = slab * tiles
    start = lax.axis_index("tile") * slab
    parity = lax.axis_index("view") % 2
    columns = jnp.arange(depth_cells, dtype=jnp.int32)
    matrix = jnp.sum(weight[:, :, None] * (index[:, :, None] == columns[None, None, :]), axis=1)
    label_ext = extended(region, (("tile", 0),), SWEEPS)
    views = lax.axis_size("view")
    half_turn = [
        (v * tiles + t, (v + 2) % views * tiles + tiles - 1 - t)
        for v in range(views)
        for t in range(tiles)
    ]
    current = recorded
    for step in range(ITERS):
        forward_flat = jnp.dot(
            current.reshape(-1, depth_cells), matrix.T, precision=lax.Precision.HIGHEST
        )
        field = recorded / forward_flat.reshape(current.shape)
        flat = jnp.dot(field.reshape(-1, depth_cells), matrix, precision=lax.Precision.HIGHEST)
        correction = flat.reshape(field.shape)
        turned = jnp.flip(lax.ppermute(correction, ("view", "tile"), half_turn), (0, 2))
        paired = jnp.sqrt(correction * turned)
        outgoing = jnp.where(parity == 0, jnp.flip(paired, 2), paired)
        rotated = regroup(
            lax.all_to_all(outgoing, "tile", split_axis=2, concat_axis=2, tiled=True), tiles
        )
        rotated = jnp.where(parity == 1, jnp.flip(rotated, 2), rotated)
        partner = swapped(rotated, "view", 0)
        current = current * jnp.sqrt(paired * partner)
        widened = extended(current, (("tile", 0),), SWEEPS)
        for sweep in range(SWEEPS):
            extent = widened.shape[0]
            widened = sweep_rows(
                widened,
                label_ext[sweep : sweep + extent],
                start - SWEEPS + sweep,
                total_rows,
            )
        current = widened
    return current[None]


def rows_reversed():
    v = lax.axis_index("view")
    return lax.rem(v + 1, VIEWS) >= 2


def depth_reversed():
    return lax.axis_index("view") >= 2


def own_slot(tiles):
    t = lax.axis_index("tile")
    return jnp.where(rows_reversed(), tiles - 1 - t, t)


def lane_order(shape, depth_cells):
    lane = lax.broadcasted_iota(jnp.int32, shape, 1)
    base = lane // depth_cells * depth_cells
    return jnp.where(depth_reversed(), base + (base + depth_cells - 1 - lane), lane)


def pack_one(source, held, target, groups):
    slab, rows, depth_cells = held.shape
    turn = rows_reversed()
    for i in range(slab):
        held[i] = source[0, jnp.where(turn, slab - 1 - i, i)]
    part = rows // groups
    cells = jnp.swapaxes(held[...], 0, 1)
    cells = jnp.concatenate([cells[g * part : (g + 1) * part] for g in range(groups)], axis=2)
    flat = cells.reshape(part * slab, groups * depth_cells)
    order = lane_order(flat.shape, depth_cells)
    flat = jnp.take_along_axis(flat, order, axis=1)
    target[...] = flat.reshape(target.shape).astype(target.dtype)


def pack_kernel(groups, data, labels, data_out, both_out, held, held_labels):
    pack_one(data, held, data_out, groups)
    part = data_out.shape[0]
    both_out[:part] = data_out[...]
    pack_one(labels, held_labels, both_out.at[part:], groups)


def split(cells):
    high = cells.astype(jnp.bfloat16)
    return high, (cells - high.astype(jnp.float32)).astype(jnp.bfloat16)


def band_kernel(kernel, offsets, blur_out, adjoint_out, turned_out):
    depth_cells, taps = kernel.shape[1:]
    span = blur_out.shape[0] // 2
    turn = depth_reversed()
    row = lax.broadcasted_iota(jnp.int32, (depth_cells, depth_cells), 0)
    col = lax.broadcasted_iota(jnp.int32, (depth_cells, depth_cells), 1)
    pick = col == jnp.where(turn, depth_cells - 1 - row, row)
    shift = jnp.sum(
        jnp.where(pick, jnp.broadcast_to(offsets[...], pick.shape), 0), axis=1, keepdims=True
    )
    depth = row[:, :1]
    depth = jnp.where(turn, depth_cells - 1 - depth, depth)
    taps_by_row = jnp.dot(
        pick.astype(jnp.float32),
        kernel[0],
        precision=lax.Precision.HIGHEST,
        preferred_element_type=jnp.float32,
    )
    weight = taps_by_row / jnp.sum(taps_by_row, axis=1, keepdims=True)
    lane = lax.broadcasted_iota(jnp.int32, (depth_cells, span), 1)
    within = lax.rem(lane, depth_cells)
    within = jnp.where(turn, depth_cells - 1 - within, within)
    total = jnp.zeros((depth_cells, span), jnp.float32)
    for k in range(taps):
        index = jnp.clip(depth + (k - 4) + shift, 0, depth_cells - 1)
        total = total + jnp.where(index == within, weight[:, k : k + 1], 0.0)
    matrix = jnp.concatenate(
        [jnp.where(lane // depth_cells == g, total, 0.0) for g in range(span // depth_cells)], axis=0
    )
    for cells, out in ((matrix.T, blur_out), (matrix, adjoint_out)):
        high, low = split(cells)
        for half in range(2):
            out[half * span : (half + 1) * span, :span] = high
            out[half * span : (half + 1) * span, span:] = low
    for half, cells in enumerate(split(matrix.T)):
        turned_out[half * span : (half + 1) * span, :span] = cells
        turned_out[half * span : (half + 1) * span, span:] = cells


def banded(cells, band):
    high, low = split(cells)
    both = jnp.dot(
        jnp.concatenate([high, low], axis=1), band[...], preferred_element_type=jnp.float32
    )
    lanes = cells.shape[1]
    return both[:, :lanes] + both[:, lanes:]


def corrected(recorded, estimate, blur_band, adjoint_band):
    return banded(recorded / banded(estimate, blur_band), adjoint_band)


def first_correction(block, blur_band, adjoint_band):
    flat = block.reshape(-1, block.shape[-1])
    return corrected(flat, flat, blur_band, adjoint_band).reshape(block.shape)


def place(target, slot, block):
    slab = block.shape[1]
    target[:, pl.ds(pl.multiple_of(slot * slab, slab), slab), :] = block


def blocks_kernel(blur_band, adjoint_band, *refs):
    blocks, correction = refs[:-1], refs[-1]
    part = correction.shape[0] // len(blocks)
    cells = jnp.concatenate([block[:part] for block in blocks], axis=0)
    correction[...] = first_correction(cells, blur_band, adjoint_band)


def relay_kernel(own_both, both, labels_out):
    part = both.shape[0] // 2
    labels_out[:part] = own_both[part:]
    labels_out[part:] = both[part:]


def pair_kernel(tiles, *refs):
    own, far, products = refs[:2], refs[2:4], refs[4:]
    pair = own[0].shape[0]
    part = pair // 2
    slot = own_slot(tiles)
    for k in range(tiles):
        mine, theirs = k * part, (tiles - 1 - k) * part
        near = own[mine // pair][mine % pair : mine % pair + part]
        cells = near * far[theirs // pair][theirs % pair : theirs % pair + part]
        for i, product in enumerate(products):
            size = product.shape[0]
            place(product, slot ^ k, cells[i * size : (i + 1) * size])


def recorded_kernel(tiles, *refs):
    blocks, recorded = refs[:-1], refs[-1]
    slot = own_slot(tiles)
    for k, ref in enumerate(blocks):
        place(recorded, slot ^ k, ref[: recorded.shape[0]])


def weights_kernel(tiles, depth_cells, near, far, *refs):
    outs, whole = refs[:-1], refs[-1]
    slot = own_slot(tiles)
    slab, lanes = near.shape[1:]
    part = near.shape[0] // 2
    for k in range(tiles):
        if k in (0, LABELS_WITH):
            cells = near[part:] if k else near[:part]
        else:
            cells = far[:part] if k == LABELS_BY else far[part:]
        place(whole, slot ^ k, cells)
    total_rows = tiles * slab
    region = whole[...].reshape(part * total_rows, lanes)
    row = lax.broadcasted_iota(jnp.int32, region.shape, 0)
    lane = lax.broadcasted_iota(jnp.int32, region.shape, 1)

    def weighted(upper, inside):
        same = jnp.where(upper == region, TAU, TAU * WEAK)
        return jnp.where(inside, same, 0.0)

    along_x = weighted(up_rows(region), lax.rem(row, total_rows) != total_rows - 1)
    along_y = weighted(
        up_second(region, total_rows, depth_cells),
        (row < (part - 1) * total_rows) | (lane < lanes - depth_cells),
    )
    along_z = weighted(up_depth(region), lax.rem(lane, depth_cells) != depth_cells - 1)
    shares = [
        along_x,
        down_rows(along_x),
        along_y,
        down_second(along_y, total_rows, depth_cells),
        along_z,
        down_depth(along_z),
    ]
    shares.append(1.0 - sum(shares[1:], shares[0]))
    for share, out in zip(shares, outs):
        out[...] = share.reshape(out.shape)


def up_rows(cells):
    return pltpu.roll(cells, cells.shape[0] - 1, 0)


def up_depth(cells):
    return pltpu.roll(cells, cells.shape[1] - 1, 1)


def up_second(cells, total_rows, depth_cells):
    first = pltpu.roll(cells[:total_rows], cells.shape[1] - depth_cells, 1)
    return jnp.concatenate([cells[total_rows:], first], axis=0)


def down_second(cells, total_rows, depth_cells):
    last = pltpu.roll(cells[-total_rows:], depth_cells, 1)
    return jnp.concatenate([last, cells[:-total_rows]], axis=0)


def down_rows(cells):
    return pltpu.roll(cells, 1, 0)


def down_depth(cells):
    return pltpu.roll(cells, 1, 1)


def swept(cells, shares, held, total_rows, depth_cells):
    up_x, down_x, up_y, down_y, up_z, down_z, kept = [
        ref[...].reshape(cells.shape) for ref in shares
    ]
    rows = cells.shape[0]
    held[ROWS : ROWS + rows] = cells
    return (
        (up_z * up_depth(cells) + down_z * down_depth(cells))
        + (up_x * held[ROWS + 1 : ROWS + 1 + rows] + down_x * held[ROWS - 1 : ROWS - 1 + rows])
        + (
            up_y * up_second(cells, total_rows, depth_cells)
            + down_y * down_second(cells, total_rows, depth_cells)
        )
        + kept * cells
    )


def exchanged(cells, depth_cells):
    part, rows, lanes = cells.shape
    groups = lanes // depth_cells
    turned = [
        cells[first : first + groups].reshape(groups * rows, lanes).T
        for first in range(0, part, groups)
    ]
    return regrouped(turned, rows, depth_cells)


def regrouped(turned, rows, depth_cells):
    lanes = turned[0].shape[1]
    groups = lanes // depth_cells
    lane_group = lax.broadcasted_iota(jnp.int32, (rows, lanes), 1) // depth_cells
    out = []
    for cells in turned:
        for a in range(groups):
            plane = None
            for b in range(groups):
                piece = cells[b * rows : (b + 1) * rows]
                moved = (b - a) % groups * depth_cells
                if moved:
                    piece = pltpu.roll(piece, moved, 1)
                plane = piece if plane is None else jnp.where(lane_group == b, piece, plane)
            out.append(plane)
    return jnp.stack(out)


def window(ref, slot, tiles, slab, margin):
    parts = []
    for step in (-1, 0, 1):
        at = lax.rem(slot + step + tiles, tiles) * slab
        parts.append(ref[:, pl.ds(pl.multiple_of(at, slab), slab), :])
    return jnp.concatenate(parts, axis=1)[:, slab - margin : 2 * slab + margin, :]


def second_kernel(
    depth_cells,
    blur_band,
    adjoint_band,
    turned_band,
    recorded,
    *refs,
):
    refs, (estimate, correction, turned, shifted) = refs[:-4], refs[-4:]
    shifted[:ROWS] = jnp.zeros_like(shifted[:ROWS])
    shifted[-ROWS:] = jnp.zeros_like(shifted[-ROWS:])
    pieces, shares = refs[:-SHARES], refs[-SHARES:]
    pairs = len(pieces) // 2
    part, total_rows, lanes = recorded.shape
    flat = (part * total_rows, lanes)
    own, other = [
        jnp.concatenate([piece[...] for piece in half], axis=0)
        for half in (pieces[:pairs], pieces[pairs:])
    ]
    joined = lax.rsqrt(lax.rsqrt(own * exchanged(other, depth_cells)))
    cells = (recorded[...] * joined).reshape(flat)
    for _ in range(SWEEPS):
        cells = swept(cells, shares, shifted, total_rows, depth_cells)
    estimate[...] = cells.reshape(estimate.shape)
    ratio = recorded[...].reshape(flat) / banded(cells, blur_band)
    both = lax.dot_general(
        turned_band[...],
        jnp.concatenate(split(ratio), axis=1),
        (((1,), (1,)), ((), ())),
        preferred_element_type=jnp.float32,
    )
    both = both[:lanes] + both[lanes:]
    both = [both[:, first : first + lanes] for first in range(0, both.shape[1], lanes)]
    turned[...] = regrouped(both, total_rows, depth_cells)
    correction[...] = banded(ratio, adjoint_band).reshape(correction.shape)


def windows_kernel(tiles, own, other, sent, product):
    product[...] = own[...] * other[...]
    slab = product.shape[1] // tiles
    sent[...] = window(product, tiles - 1 - own_slot(tiles), tiles, slab, SWEEPS)


def near_kernel(tiles, *refs):
    slot = own_slot(tiles)
    slab = refs[0].shape[1] // tiles
    half = len(refs) // 2
    for ref, out in zip(refs[:half], refs[half:]):
        out[...] = window(ref, slot, tiles, slab, SWEEPS)


def last_kernel(groups, depth_cells, estimate, kept, received, *refs):
    *shares, out, held, shifted = refs
    shifted[:ROWS] = jnp.zeros_like(shifted[:ROWS])
    shifted[-ROWS:] = jnp.zeros_like(shifted[-ROWS:])
    part, extent, lanes = estimate.shape
    slab = extent - 2 * SWEEPS
    flat = (part * extent, lanes)
    joined = lax.rsqrt(lax.rsqrt(kept[...] * received[...]))
    cells = (estimate[...] * joined).reshape(flat)
    for _ in range(SWEEPS):
        cells = swept(cells, shares, shifted, extent, depth_cells)
    cells = cells.reshape(part, extent, lanes)[:, SWEEPS : SWEEPS + slab]
    cells = cells.reshape(part * slab, lanes)
    cells = jnp.take_along_axis(cells, lane_order(cells.shape, depth_cells), axis=1)
    cells = cells.reshape(part, slab, lanes)
    cells = jnp.concatenate(
        [cells[:, :, g * depth_cells : (g + 1) * depth_cells] for g in range(groups)], axis=0
    )
    held[...] = jnp.swapaxes(cells, 0, 1)
    turn = rows_reversed()
    for i in range(slab):
        out[0, i] = held[jnp.where(turn, slab - 1 - i, i)]


def whole_views(data, labels, kernel, offsets):
    tiles = lax.axis_size("tile")
    _, slab, rows, depth_cells = data.shape
    groups = LANES // depth_cells
    part = rows // groups
    total_rows = slab * tiles
    extent = slab + 2 * SWEEPS
    f32 = jnp.float32
    block = (part, slab, LANES)
    view = (part, total_rows, LANES)
    near = (part, extent, LANES)
    vmem = pl.BlockSpec(memory_space=pltpu.VMEM)

    def call(body, outs, scratch, *args):
        shapes = tuple(jax.ShapeDtypeStruct(s, d) for s, d in outs)
        return pl.pallas_call(
            body,
            out_shape=shapes,
            in_specs=[vmem] * len(args),
            out_specs=tuple(vmem for _ in shapes),
            scratch_shapes=scratch,
            compiler_params=pltpu.CompilerParams(vmem_limit_bytes=32 << 20),
        )(*args)

    def across(cells, k):
        return lax.ppermute(cells, "tile", [(i, i ^ k) for i in range(tiles)])

    def swap(cells, bit):
        return lax.ppermute(cells, "view", [(i, i ^ bit) for i in range(VIEWS)])

    packed, both = call(
        functools.partial(pack_kernel, groups),
        [(block, f32), ((2 * part,) + block[1:], f32)],
        [pltpu.VMEM(data.shape[1:], f32), pltpu.VMEM(data.shape[1:], jnp.int32)],
        data,
        labels,
    )
    *bands, turned_band = call(
        band_kernel, [((2 * LANES, 2 * LANES), jnp.bfloat16)] * 3, [], kernel, offsets
    )
    blocks = [packed] + [across(both if k == LABELS_WITH else packed, k) for k in range(1, tiles)]
    two = ((2 * part,) + block[1:], f32)
    (near_labels,) = call(relay_kernel, [two], [], both, blocks[LABELS_WITH])
    made = [
        call(blocks_kernel, [two], [], *bands, *blocks[:2])[0],
        call(blocks_kernel, [two], [], *bands, *blocks[2:])[0],
    ]
    opposite = [swap(cells, 2) for cells in made]
    pieces = 2
    products = call(
        functools.partial(pair_kernel, tiles),
        [((part // pieces,) + view[1:], f32)] * pieces,
        [],
        *made,
        *opposite,
    )
    (recorded,) = call(
        functools.partial(recorded_kernel, tiles),
        [(view, f32)],
        [],
        *blocks,
    )
    far_labels = across(near_labels, LABELS_BY)
    others = [swap(product, 1) for product in products]
    shares = call(
        functools.partial(weights_kernel, tiles, depth_cells),
        [(view, f32)] * SHARES,
        [pltpu.VMEM(view, f32)],
        near_labels,
        far_labels,
    )
    estimate, correction, turned = call(
        functools.partial(second_kernel, depth_cells),
        [(view, f32)] * 3,
        [pltpu.VMEM((part * total_rows + 2 * ROWS, LANES), f32)],
        *bands,
        turned_band,
        recorded,
        *products,
        *others,
        *shares,
    )
    other = swap(turned, 1)
    sent, product = call(
        functools.partial(windows_kernel, tiles),
        [(near, f32), (view, f32)],
        [],
        correction,
        other,
    )
    kept, *near_cells = call(
        functools.partial(near_kernel, tiles),
        [(near, f32)] * (2 + SHARES),
        [],
        product,
        estimate,
        *shares,
    )
    received = swap(sent, 2)
    (out,) = call(
        functools.partial(last_kernel, groups, depth_cells),
        [(data.shape, f32)],
        [pltpu.VMEM(data.shape[1:], f32), pltpu.VMEM((part * extent + 2 * ROWS, LANES), f32)],
        near_cells[0],
        kept,
        received,
        *near_cells[1:],
    )
    return out


def fits_whole(shape):
    _, slab, rows, depth_cells = shape
    tiles = lax.axis_size("tile")
    return (
        lax.axis_size("view") == VIEWS
        and ITERS == 2
        and slab % ROWS == 0
        and slab >= SWEEPS
        and slab * tiles == depth_cells
        and tiles == 4
        and LANES % depth_cells == 0
        and rows % (LANES // depth_cells) ** 2 == 0
        and (2 * SWEEPS) % ROWS == 0
    )


def on_device(data, labels, kernel, offsets):
    form = whole_views if fits_whole(data.shape) else by_slabs
    return form(data, labels, kernel, offsets)


def solution(mesh):
    placed = (
        P(("parts", "view"), "tile", None, None),
        P(("parts", "view"), "tile", None, None),
        P("view", None, None),
        P("view", None),
    )
    return jax.shard_map(
        on_device,
        mesh=mesh,
        in_specs=placed,
        out_specs=P(("parts", "view"), "tile", None, None),
        check_vma=False,
    )
```

```python
import functools

import jax
import jax.experimental.pallas as pl
import jax.experimental.pallas.tpu as pltpu
import jax.numpy as jnp
from jax import lax
from jax.sharding import PartitionSpec as P

ITERS = 2
SWEEPS = 4

WEAK = 0.2
TAU = 0.15

LANES = 128
ROWS = 8
VIEWS = 4
SHARES = 7

LABELS_WITH = 3
LABELS_BY = 1


def extended(cells, sides, width):
    for axis, dim in sides:
        count = lax.axis_size(axis)
        ends = count - 1
        head = lax.slice_in_dim(cells, 0, width, axis=dim)
        tail = lax.slice_in_dim(cells, cells.shape[dim] - width, cells.shape[dim], axis=dim)
        cells = jnp.concatenate(
            [
                lax.ppermute(tail, axis, [(i, (i + 1) % count) for i in range(ends)]),
                cells,
                lax.ppermute(head, axis, [((i + 1) % count, i) for i in range(ends)]),
            ],
            axis=dim,
        )
    return cells


def swapped(block, axis, stride):
    count = lax.axis_size(axis)
    route = []
    for low in range(count):
        high = low | 1 << stride
        if high != low and high < count:
            route += [(low, high), (high, low)]
    return lax.ppermute(block, axis, route)


def band(kernel, offsets):
    depth_cells = kernel.shape[0]
    taps = jnp.arange(kernel.shape[1], dtype=jnp.int32) - 4
    depth = jnp.arange(depth_cells, dtype=jnp.int32)
    index = jnp.clip(depth[:, None] + taps[None, :] + offsets[:, None], 0, depth_cells - 1)
    weight = kernel / jnp.sum(kernel, axis=1, keepdims=True)
    return (index, weight)


def axis_term(field, region, axis):
    count = field.shape[axis]
    upper = lax.slice_in_dim(field, 1, count, axis=axis)
    lower = lax.slice_in_dim(field, 0, count - 1, axis=axis)
    same = jnp.where(
        lax.slice_in_dim(region, 1, count, axis=axis)
        == lax.slice_in_dim(region, 0, count - 1, axis=axis),
        1.0,
        WEAK,
    )
    flux = same * (upper - lower)
    after = [(0, 0)] * 3
    before = [(0, 0)] * 3
    after[axis] = (0, 1)
    before[axis] = (1, 0)
    return jnp.pad(flux, after) - jnp.pad(flux, before)


def sweep_rows(field, region, first_row, total_rows):
    extent = field.shape[0]
    global_rows = first_row + jnp.arange(extent, dtype=jnp.int32)
    inside = ((global_rows >= 0) & (global_rows < total_rows)).astype(field.dtype)[:, None, None]
    same = jnp.where(region[1:] == region[:-1], 1.0, WEAK) * inside[1:] * inside[:-1]
    flux = same * (field[1:] - field[:-1])
    inner = field[1:-1]
    inner_labels = region[1:-1]
    total = (
        flux[1:] - flux[:-1] + axis_term(inner, inner_labels, 1) + axis_term(inner, inner_labels, 2)
    )
    return inner + TAU * total


def regroup(received, tiles):
    slab, rows, depth_cells = received.shape
    blocks = received.reshape(slab, rows, tiles, depth_cells // tiles)
    return blocks.transpose(3, 1, 2, 0).reshape(depth_cells // tiles, rows, depth_cells)


def by_slabs(data, labels, kernel, offsets):
    recorded = data[0]
    region = labels[0]
    index, weight = band(kernel[0], offsets[0])
    tiles = lax.axis_size("tile")
    slab, rows, depth_cells = recorded.shape
    total_rows = slab * tiles
    start = lax.axis_index("tile") * slab
    parity = lax.axis_index("view") % 2
    columns = jnp.arange(depth_cells, dtype=jnp.int32)
    matrix = jnp.sum(weight[:, :, None] * (index[:, :, None] == columns[None, None, :]), axis=1)
    label_ext = extended(region, (("tile", 0),), SWEEPS)
    views = lax.axis_size("view")
    half_turn = [
        (v * tiles + t, (v + 2) % views * tiles + tiles - 1 - t)
        for v in range(views)
        for t in range(tiles)
    ]
    current = recorded
    for step in range(ITERS):
        forward_flat = jnp.dot(
            current.reshape(-1, depth_cells), matrix.T, precision=lax.Precision.HIGHEST
        )
        field = recorded / forward_flat.reshape(current.shape)
        flat = jnp.dot(field.reshape(-1, depth_cells), matrix, precision=lax.Precision.HIGHEST)
        correction = flat.reshape(field.shape)
        turned = jnp.flip(lax.ppermute(correction, ("view", "tile"), half_turn), (0, 2))
        paired = jnp.sqrt(correction * turned)
        outgoing = jnp.where(parity == 0, jnp.flip(paired, 2), paired)
        rotated = regroup(
            lax.all_to_all(outgoing, "tile", split_axis=2, concat_axis=2, tiled=True), tiles
        )
        rotated = jnp.where(parity == 1, jnp.flip(rotated, 2), rotated)
        partner = swapped(rotated, "view", 0)
        current = current * jnp.sqrt(paired * partner)
        widened = extended(current, (("tile", 0),), SWEEPS)
        for sweep in range(SWEEPS):
            extent = widened.shape[0]
            widened = sweep_rows(
                widened,
                label_ext[sweep : sweep + extent],
                start - SWEEPS + sweep,
                total_rows,
            )
        current = widened
    return current[None]


def rows_reversed():
    v = lax.axis_index("view")
    return lax.rem(v + 1, VIEWS) >= 2


def depth_reversed():
    return lax.axis_index("view") >= 2


def own_slot(tiles):
    t = lax.axis_index("tile")
    return jnp.where(rows_reversed(), tiles - 1 - t, t)


def lane_order(shape, depth_cells):
    lane = lax.broadcasted_iota(jnp.int32, shape, 1)
    base = lane // depth_cells * depth_cells
    return jnp.where(depth_reversed(), base + (base + depth_cells - 1 - lane), lane)


def pack_one(source, held, target, groups):
    slab, rows, depth_cells = held.shape
    turn = rows_reversed()
    for i in range(slab):
        held[i] = source[0, jnp.where(turn, slab - 1 - i, i)]
    part = rows // groups
    cells = jnp.swapaxes(held[...], 0, 1)
    cells = jnp.concatenate([cells[g * part : (g + 1) * part] for g in range(groups)], axis=2)
    flat = cells.reshape(part * slab, groups * depth_cells)
    order = lane_order(flat.shape, depth_cells)
    flat = jnp.take_along_axis(flat, order, axis=1)
    target[...] = flat.reshape(target.shape).astype(target.dtype)


def pack_kernel(groups, data, labels, data_out, both_out, held, held_labels):
    pack_one(data, held, data_out, groups)
    part = data_out.shape[0]
    both_out[:part] = data_out[...]
    pack_one(labels, held_labels, both_out.at[part:], groups)


def split(cells):
    high = cells.astype(jnp.bfloat16)
    return high, (cells - high.astype(jnp.float32)).astype(jnp.bfloat16)


def band_kernel(kernel, offsets, blur_out, adjoint_out, turned_out):
    depth_cells, taps = kernel.shape[1:]
    span = blur_out.shape[0] // 2
    turn = depth_reversed()
    row = lax.broadcasted_iota(jnp.int32, (depth_cells, depth_cells), 0)
    col = lax.broadcasted_iota(jnp.int32, (depth_cells, depth_cells), 1)
    pick = col == jnp.where(turn, depth_cells - 1 - row, row)
    shift = jnp.sum(
        jnp.where(pick, jnp.broadcast_to(offsets[...], pick.shape), 0), axis=1, keepdims=True
    )
    depth = row[:, :1]
    depth = jnp.where(turn, depth_cells - 1 - depth, depth)
    taps_by_row = jnp.dot(
        pick.astype(jnp.float32),
        kernel[0],
        precision=lax.Precision.HIGHEST,
        preferred_element_type=jnp.float32,
    )
    weight = taps_by_row / jnp.sum(taps_by_row, axis=1, keepdims=True)
    lane = lax.broadcasted_iota(jnp.int32, (depth_cells, span), 1)
    within = lax.rem(lane, depth_cells)
    within = jnp.where(turn, depth_cells - 1 - within, within)
    total = jnp.zeros((depth_cells, span), jnp.float32)
    for k in range(taps):
        index = jnp.clip(depth + (k - 4) + shift, 0, depth_cells - 1)
        total = total + jnp.where(index == within, weight[:, k : k + 1], 0.0)
    matrix = jnp.concatenate(
        [jnp.where(lane // depth_cells == g, total, 0.0) for g in range(span // depth_cells)], axis=0
    )
    for cells, out in ((matrix.T, blur_out), (matrix, adjoint_out)):
        high, low = split(cells)
        for half in range(2):
            out[half * span : (half + 1) * span, :span] = high
            out[half * span : (half + 1) * span, span:] = low
    for half, cells in enumerate(split(matrix.T)):
        turned_out[half * span : (half + 1) * span, :span] = cells
        turned_out[half * span : (half + 1) * span, span:] = cells


def banded(cells, band):
    high, low = split(cells)
    both = jnp.dot(
        jnp.concatenate([high, low], axis=1), band[...], preferred_element_type=jnp.float32
    )
    lanes = cells.shape[1]
    return both[:, :lanes] + both[:, lanes:]


def corrected(recorded, estimate, blur_band, adjoint_band):
    return banded(recorded * pl.reciprocal(banded(estimate, blur_band)), adjoint_band)


def first_correction(block, blur_band, adjoint_band):
    flat = block.reshape(-1, block.shape[-1])
    return corrected(flat, flat, blur_band, adjoint_band).reshape(block.shape)


def place(target, slot, block):
    slab = block.shape[1]
    target[:, pl.ds(pl.multiple_of(slot * slab, slab), slab), :] = block


def blocks_kernel(blur_band, adjoint_band, *refs):
    blocks, correction = refs[:-1], refs[-1]
    part = correction.shape[0] // len(blocks)
    cells = jnp.concatenate([block[:part] for block in blocks], axis=0)
    correction[...] = first_correction(cells, blur_band, adjoint_band)


def relay_kernel(own_both, both, labels_out):
    part = both.shape[0] // 2
    labels_out[:part] = own_both[part:]
    labels_out[part:] = both[part:]


def pair_kernel(tiles, *refs):
    own, far, products = refs[:2], refs[2:4], refs[4:]
    pair = own[0].shape[0]
    part = pair // 2
    slot = own_slot(tiles)
    for k in range(tiles):
        mine, theirs = k * part, (tiles - 1 - k) * part
        near = own[mine // pair][mine % pair : mine % pair + part]
        cells = near * far[theirs // pair][theirs % pair : theirs % pair + part]
        for i, product in enumerate(products):
            size = product.shape[0]
            place(product, slot ^ k, cells[i * size : (i + 1) * size])


def recorded_kernel(tiles, *refs):
    blocks, recorded = refs[:-1], refs[-1]
    slot = own_slot(tiles)
    for k, ref in enumerate(blocks):
        place(recorded, slot ^ k, ref[: recorded.shape[0]])


def weights_kernel(tiles, depth_cells, near, far, *refs):
    outs, whole = refs[:-1], refs[-1]
    slot = own_slot(tiles)
    slab, lanes = near.shape[1:]
    part = near.shape[0] // 2
    for k in range(tiles):
        if k in (0, LABELS_WITH):
            cells = near[part:] if k else near[:part]
        else:
            cells = far[:part] if k == LABELS_BY else far[part:]
        place(whole, slot ^ k, cells)
    total_rows = tiles * slab
    region = whole[...].reshape(part * total_rows, lanes)
    row = lax.broadcasted_iota(jnp.int32, region.shape, 0)
    lane = lax.broadcasted_iota(jnp.int32, region.shape, 1)

    def weighted(upper, inside):
        same = jnp.where(upper == region, TAU, TAU * WEAK)
        return jnp.where(inside, same, 0.0)

    along_x = weighted(up_rows(region), lax.rem(row, total_rows) != total_rows - 1)
    along_y = weighted(
        up_second(region, total_rows, depth_cells),
        (row < (part - 1) * total_rows) | (lane < lanes - depth_cells),
    )
    along_z = weighted(up_depth(region), lax.rem(lane, depth_cells) != depth_cells - 1)
    shares = [
        along_x,
        down_rows(along_x),
        along_y,
        down_second(along_y, total_rows, depth_cells),
        along_z,
        down_depth(along_z),
    ]
    shares.append(1.0 - sum(shares[1:], shares[0]))
    for share, out in zip(shares, outs):
        out[...] = share.reshape(out.shape)


def up_rows(cells):
    return pltpu.roll(cells, cells.shape[0] - 1, 0)


def up_depth(cells):
    return pltpu.roll(cells, cells.shape[1] - 1, 1)


def up_second(cells, total_rows, depth_cells):
    first = pltpu.roll(cells[:total_rows], cells.shape[1] - depth_cells, 1)
    return jnp.concatenate([cells[total_rows:], first], axis=0)


def down_second(cells, total_rows, depth_cells):
    last = pltpu.roll(cells[-total_rows:], depth_cells, 1)
    return jnp.concatenate([last, cells[:-total_rows]], axis=0)


def down_rows(cells):
    return pltpu.roll(cells, 1, 0)


def down_depth(cells):
    return pltpu.roll(cells, 1, 1)


def swept(cells, shares, held, total_rows, depth_cells):
    up_x, down_x, up_y, down_y, up_z, down_z, kept = [
        ref[...].reshape(cells.shape) for ref in shares
    ]
    rows = cells.shape[0]
    held[ROWS : ROWS + rows] = cells
    return (
        (up_z * up_depth(cells) + down_z * down_depth(cells))
        + (up_x * held[ROWS + 1 : ROWS + 1 + rows] + down_x * held[ROWS - 1 : ROWS - 1 + rows])
        + (
            up_y * up_second(cells, total_rows, depth_cells)
            + down_y * down_second(cells, total_rows, depth_cells)
        )
        + kept * cells
    )


def exchanged(cells, depth_cells):
    part, rows, lanes = cells.shape
    groups = lanes // depth_cells
    turned = [
        cells[first : first + groups].reshape(groups * rows, lanes).T
        for first in range(0, part, groups)
    ]
    return regrouped(turned, rows, depth_cells)


def regrouped(turned, rows, depth_cells):
    lanes = turned[0].shape[1]
    groups = lanes // depth_cells
    lane_group = lax.broadcasted_iota(jnp.int32, (rows, lanes), 1) // depth_cells
    out = []
    for cells in turned:
        for a in range(groups):
            plane = None
            for b in range(groups):
                piece = cells[b * rows : (b + 1) * rows]
                moved = (b - a) % groups * depth_cells
                if moved:
                    piece = pltpu.roll(piece, moved, 1)
                plane = piece if plane is None else jnp.where(lane_group == b, piece, plane)
            out.append(plane)
    return jnp.stack(out)


def window(ref, slot, tiles, slab, margin):
    parts = []
    for step in (-1, 0, 1):
        at = lax.rem(slot + step + tiles, tiles) * slab
        parts.append(ref[:, pl.ds(pl.multiple_of(at, slab), slab), :])
    return jnp.concatenate(parts, axis=1)[:, slab - margin : 2 * slab + margin, :]


def second_kernel(
    depth_cells,
    blur_band,
    adjoint_band,
    turned_band,
    recorded,
    *refs,
):
    refs, (estimate, correction, turned, shifted) = refs[:-4], refs[-4:]
    shifted[:ROWS] = jnp.zeros_like(shifted[:ROWS])
    shifted[-ROWS:] = jnp.zeros_like(shifted[-ROWS:])
    pieces, shares = refs[:-SHARES], refs[-SHARES:]
    pairs = len(pieces) // 2
    part, total_rows, lanes = recorded.shape
    flat = (part * total_rows, lanes)
    own, other = [
        jnp.concatenate([piece[...] for piece in half], axis=0)
        for half in (pieces[:pairs], pieces[pairs:])
    ]
    joined = lax.rsqrt(lax.rsqrt(own * exchanged(other, depth_cells)))
    cells = (recorded[...] * joined).reshape(flat)
    for _ in range(SWEEPS):
        cells = swept(cells, shares, shifted, total_rows, depth_cells)
    estimate[...] = cells.reshape(estimate.shape)
    ratio = recorded[...].reshape(flat) * pl.reciprocal(banded(cells, blur_band))
    both = lax.dot_general(
        turned_band[...],
        jnp.concatenate(split(ratio), axis=1),
        (((1,), (1,)), ((), ())),
        preferred_element_type=jnp.float32,
    )
    both = both[:lanes] + both[lanes:]
    both = [both[:, first : first + lanes] for first in range(0, both.shape[1], lanes)]
    turned[...] = regrouped(both, total_rows, depth_cells)
    correction[...] = banded(ratio, adjoint_band).reshape(correction.shape)


def windows_kernel(tiles, own, other, sent, product):
    product[...] = own[...] * other[...]
    slab = product.shape[1] // tiles
    sent[...] = window(product, tiles - 1 - own_slot(tiles), tiles, slab, SWEEPS)


def near_kernel(tiles, *refs):
    slot = own_slot(tiles)
    slab = refs[0].shape[1] // tiles
    half = len(refs) // 2
    for ref, out in zip(refs[:half], refs[half:]):
        out[...] = window(ref, slot, tiles, slab, SWEEPS)


def last_kernel(groups, depth_cells, estimate, kept, received, *refs):
    *shares, out, held, shifted = refs
    shifted[:ROWS] = jnp.zeros_like(shifted[:ROWS])
    shifted[-ROWS:] = jnp.zeros_like(shifted[-ROWS:])
    part, extent, lanes = estimate.shape
    slab = extent - 2 * SWEEPS
    flat = (part * extent, lanes)
    joined = lax.rsqrt(lax.rsqrt(kept[...] * received[...]))
    cells = (estimate[...] * joined).reshape(flat)
    for _ in range(SWEEPS):
        cells = swept(cells, shares, shifted, extent, depth_cells)
    cells = cells.reshape(part, extent, lanes)[:, SWEEPS : SWEEPS + slab]
    cells = cells.reshape(part * slab, lanes)
    cells = jnp.take_along_axis(cells, lane_order(cells.shape, depth_cells), axis=1)
    cells = cells.reshape(part, slab, lanes)
    cells = jnp.concatenate(
        [cells[:, :, g * depth_cells : (g + 1) * depth_cells] for g in range(groups)], axis=0
    )
    held[...] = jnp.swapaxes(cells, 0, 1)
    turn = rows_reversed()
    for i in range(slab):
        out[0, i] = held[jnp.where(turn, slab - 1 - i, i)]


def whole_views(data, labels, kernel, offsets):
    tiles = lax.axis_size("tile")
    _, slab, rows, depth_cells = data.shape
    groups = LANES // depth_cells
    part = rows // groups
    total_rows = slab * tiles
    extent = slab + 2 * SWEEPS
    f32 = jnp.float32
    block = (part, slab, LANES)
    view = (part, total_rows, LANES)
    near = (part, extent, LANES)
    vmem = pl.BlockSpec(memory_space=pltpu.VMEM)

    def call(body, outs, scratch, *args):
        shapes = tuple(jax.ShapeDtypeStruct(s, d) for s, d in outs)
        return pl.pallas_call(
            body,
            out_shape=shapes,
            in_specs=[vmem] * len(args),
            out_specs=tuple(vmem for _ in shapes),
            scratch_shapes=scratch,
            compiler_params=pltpu.CompilerParams(vmem_limit_bytes=32 << 20),
        )(*args)

    def across(cells, k):
        return lax.ppermute(cells, "tile", [(i, i ^ k) for i in range(tiles)])

    def swap(cells, bit):
        return lax.ppermute(cells, "view", [(i, i ^ bit) for i in range(VIEWS)])

    packed, both = call(
        functools.partial(pack_kernel, groups),
        [(block, f32), ((2 * part,) + block[1:], f32)],
        [pltpu.VMEM(data.shape[1:], f32), pltpu.VMEM(data.shape[1:], jnp.int32)],
        data,
        labels,
    )
    *bands, turned_band = call(
        band_kernel, [((2 * LANES, 2 * LANES), jnp.bfloat16)] * 3, [], kernel, offsets
    )
    blocks = [packed] + [across(both if k == LABELS_WITH else packed, k) for k in range(1, tiles)]
    two = ((2 * part,) + block[1:], f32)
    (near_labels,) = call(relay_kernel, [two], [], both, blocks[LABELS_WITH])
    made = [
        call(blocks_kernel, [two], [], *bands, *blocks[:2])[0],
        call(blocks_kernel, [two], [], *bands, *blocks[2:])[0],
    ]
    opposite = [swap(cells, 2) for cells in made]
    pieces = 2
    products = call(
        functools.partial(pair_kernel, tiles),
        [((part // pieces,) + view[1:], f32)] * pieces,
        [],
        *made,
        *opposite,
    )
    (recorded,) = call(
        functools.partial(recorded_kernel, tiles),
        [(view, f32)],
        [],
        *blocks,
    )
    far_labels = across(near_labels, LABELS_BY)
    others = [swap(product, 1) for product in products]
    shares = call(
        functools.partial(weights_kernel, tiles, depth_cells),
        [(view, f32)] * SHARES,
        [pltpu.VMEM(view, f32)],
        near_labels,
        far_labels,
    )
    estimate, correction, turned = call(
        functools.partial(second_kernel, depth_cells),
        [(view, f32)] * 3,
        [pltpu.VMEM((part * total_rows + 2 * ROWS, LANES), f32)],
        *bands,
        turned_band,
        recorded,
        *products,
        *others,
        *shares,
    )
    other = swap(turned, 1)
    sent, product = call(
        functools.partial(windows_kernel, tiles),
        [(near, f32), (view, f32)],
        [],
        correction,
        other,
    )
    kept, *near_cells = call(
        functools.partial(near_kernel, tiles),
        [(near, f32)] * (2 + SHARES),
        [],
        product,
        estimate,
        *shares,
    )
    received = swap(sent, 2)
    (out,) = call(
        functools.partial(last_kernel, groups, depth_cells),
        [(data.shape, f32)],
        [pltpu.VMEM(data.shape[1:], f32), pltpu.VMEM((part * extent + 2 * ROWS, LANES), f32)],
        near_cells[0],
        kept,
        received,
        *near_cells[1:],
    )
    return out


def fits_whole(shape):
    _, slab, rows, depth_cells = shape
    tiles = lax.axis_size("tile")
    return (
        lax.axis_size("view") == VIEWS
        and ITERS == 2
        and slab % ROWS == 0
        and slab >= SWEEPS
        and slab * tiles == depth_cells
        and tiles == 4
        and LANES % depth_cells == 0
        and rows % (LANES // depth_cells) ** 2 == 0
        and (2 * SWEEPS) % ROWS == 0
    )


def on_device(data, labels, kernel, offsets):
    form = whole_views if fits_whole(data.shape) else by_slabs
    return form(data, labels, kernel, offsets)


def solution(mesh):
    placed = (
        P(("parts", "view"), "tile", None, None),
        P(("parts", "view"), "tile", None, None),
        P("view", None, None),
        P("view", None),
    )
    return jax.shard_map(
        on_device,
        mesh=mesh,
        in_specs=placed,
        out_specs=P(("parts", "view"), "tile", None, None),
        check_vma=False,
    )
```
